32 devices in a mesh: attn: 8 (over z, y), proj: 4 (over x, core).
Axes of the slice: x: 2, y: 2, z: 4, core: 2. Of those that a mesh axis runs over, the one named last changes fastest.
Arguments:
- tokens: bfloat16 [4096, 4096], P('attn', 'proj'), may hold values from -6 to 6
- norm_gain: float32 [4096], replicated, may hold values from 0.1 to 1.9
- w_query: bfloat16 [4096, 4096], P(None, 'proj')
- w_key: bfloat16 [4096, 1024], P(None, 'proj')
- value_matrix: bfloat16 [4096, 1024], P(None, 'proj'), may hold values from -0.09375 to 0.09375
- doc_lengths: int32 [32], replicated, may hold values from 1 to 512, 4096 in all
- block_server: int32 [32], P('attn'), may hold values from 0 to 7, as said below
Outputs:
- attn_out: bfloat16 [4096, 4096], P('attn', 'proj')
- served_lse: float32 [32, 32, 128], P('attn', 'proj')
The draws below stay inside these ranges and needn't reach their ends.
Inputs may be any that keep to these rules, and one draw needn't show every extreme that they name: `doc_lengths`: the lengths sum to 4096. `block_server`: query block b belongs to the micro-batch b // 4; every index of attn serves exactly 4 blocks, and at most one block of any one micro-batch.
All inputs are finite; a program needn't handle non-finite values.
Results may differ from the reference program's by a relative error of at most 0.0074.
Values may be sent and summed in bfloat16 or wider, within the bound.
No kernel may reach another device: no remote copies, remote signals or barrier semaphores. Data moves between devices by JAX's collectives and lax.ppermute only.
A program may use at most 128 MiB of HBM per device.

```python
import math
import jax
import jax.numpy as jnp
import numpy as np
from jax import lax

MODEL_DIMENSION = 4096
QUERY_HEADS = 32
KEY_VALUE_HEADS = 8
HEAD_SIZE = 128
QUERY_BLOCK_ROWS = 128
BPS = 4
TOKENS = 4096
NB = 32
MAXDOC = 512
NDOCS = 32
HEADS_PER_GROUP = 4
N_ATTN = 8


def draw_tokens(key, part):
    starting_row = jax.random.normal(jax.random.fold_in(key, 22), (TOKENS, MODEL_DIMENSION), jnp.float32)
    return jnp.clip(starting_row, -6.0, 6.0).astype(jnp.bfloat16)


def grouped_keys(key):
    return jax.random.normal(jax.random.fold_in(key, 31), (MODEL_DIMENSION, KEY_VALUE_HEADS * HEAD_SIZE), jnp.float32) / MODEL_DIMENSION ** 0.5


def draw_w_key(key, part):
    return grouped_keys(key).astype(jnp.bfloat16)


def draw_w_query(key, part):
    own = jax.random.normal(jax.random.fold_in(key, 32), (MODEL_DIMENSION, QUERY_HEADS * HEAD_SIZE), jnp.float32) / MODEL_DIMENSION ** 0.5
    return own.astype(jnp.bfloat16)


def draw_block_server(key, part):
    sigma = jax.random.permutation(jax.random.fold_in(key, 41), N_ATTN)
    tau = jax.random.permutation(jax.random.fold_in(key, 42), N_ATTN)
    offsets = jax.random.permutation(jax.random.fold_in(key, 43), N_ATTN)[:BPS]
    blocks = jnp.arange(NB, dtype=jnp.int32)
    owner = blocks // BPS
    within = blocks % BPS
    return sigma[(tau[owner] + offsets[within]) % N_ATTN].astype(jnp.int32)


def shard_levels(own_key, shape, split, least, largest):
    gain, own = 1.0, jax.random.fold_in(own_key, 6)
    for position, blocks in split:
        heights = jnp.exp(jax.random.uniform(jax.random.fold_in(own, position), (blocks,), jnp.float32, least / len(split), largest / len(split)))
        gain = gain * jnp.repeat(heights, shape[position] // blocks).reshape([-1 if axis == position else 1 for axis in range(len(shape))])
    return gain


def length_profile(count, total, reach, slope):
    loads = [(1 << 20) // math.isqrt(grade ** slope) + 1 for grade in range(2, count + 1)]
    surplus, counts = total - reach - (count - 1), [1] * (count - 1)
    while surplus > 0:
        candidates = [i for i in range(count - 1) if counts[i] < reach]
        pool, remaining = sum([loads[i] for i in candidates]), surplus
        for i in candidates:
            more = min(reach - counts[i], max(1, remaining * loads[i] // pool), surplus)
            counts[i] = counts[i] + more
            surplus = surplus - more
    return np.array([reach] + counts)


def uneven_parts(rng, number_of, total, bound, skew):
    if number_of == 2:
        one = jax.random.randint(rng, (), max(1, total - bound), min(bound, total - 1) + 1)
        return jnp.stack([one, total - one])
    lengths = jnp.asarray(length_profile(number_of, total, bound, skew), jnp.int32)
    pairs = (number_of - 1) // 2
    donor, sink = lengths[1:1 + 2 * pairs:2], lengths[2:2 + 2 * pairs:2]
    margin = jnp.minimum(donor - 1, bound - sink)
    passed = jax.random.randint(jax.random.fold_in(rng, 1), (pairs,), 0, 1 << 20) % (margin + 1)
    lengths = lengths.at[1:1 + 2 * pairs:2].set(donor - passed).at[2:2 + 2 * pairs:2].set(sink + passed)
    return lengths[jax.random.permutation(jax.random.fold_in(rng, 2), number_of)]


def scatter_about(key, extent, spread, bound, pieces=(), held_as=jnp.bfloat16):
    loudness = shard_levels(key, extent, pieces, -0.22, 0.18) if pieces else 1.0
    values = jax.random.normal(key, extent, jnp.float32) * spread * loudness
    return jnp.minimum(jnp.maximum(values, -bound), bound).astype(held_as)


def setup_inputs(seed: int = 0) -> dict:
    splits = jax.random.split(jax.random.key(seed), 8)
    tokens = draw_tokens(jax.random.fold_in(splits[7], 71), 0)
    norm_gain = jnp.clip(1.0 + 0.18 * jax.random.normal(splits[1], (MODEL_DIMENSION,), jnp.float32), 0.1, 1.9)
    w_query = draw_w_query(jax.random.fold_in(splits[7], 71), 0)
    w_key = draw_w_key(jax.random.fold_in(splits[7], 71), 0)
    value_matrix = scatter_about(splits[4], (MODEL_DIMENSION, KEY_VALUE_HEADS * HEAD_SIZE), MODEL_DIMENSION ** -0.5, 0.09375, ((1, 4),))
    doc_lengths = uneven_parts(splits[5], NDOCS, TOKENS, MAXDOC, 2).astype(jnp.int32)
    block_server = draw_block_server(jax.random.fold_in(splits[7], 71), 0)
    return dict(tokens=tokens, norm_gain=norm_gain, w_query=w_query, w_key=w_key, value_matrix=value_matrix, doc_lengths=doc_lengths, block_server=block_server)


big_value = 1e+30
norm_eps = 1e-05

def reference(tokens, norm_gain, w_query, w_key, value_matrix, doc_lengths, block_server):
    inputs = tokens.astype(jnp.float32)
    inverse = lax.rsqrt(lax.optimization_barrier(jnp.sum(inputs * inputs, axis=1, keepdims=True)) / MODEL_DIMENSION + norm_eps)
    scaled = (inputs * norm_gain).astype(jnp.bfloat16)
    query_vectors = (jnp.dot(scaled, w_query, preferred_element_type=jnp.float32) * inverse).astype(jnp.bfloat16)
    keys = (jnp.dot(scaled, w_key, preferred_element_type=jnp.float32) * inverse).astype(jnp.bfloat16)
    values = (jnp.dot(scaled, value_matrix, preferred_element_type=jnp.float32) * inverse).astype(jnp.bfloat16)
    ends = jnp.cumsum(doc_lengths).astype(jnp.int32)
    starts = (ends - doc_lengths).astype(jnp.int32)
    positions = jnp.arange(TOKENS, dtype=jnp.int32)
    first = lax.optimization_barrier(jnp.max(jnp.where(starts[None, :] <= positions[:, None], starts[None, :], 0), axis=1)).astype(jnp.int32)
    padded_keys = jnp.pad(keys, ((MAXDOC, 0), (0, 0)))
    padded_values = jnp.pad(values, ((MAXDOC, 0), (0, 0)))
    row_extent = MAXDOC + QUERY_BLOCK_ROWS
    scale = 1.0 / HEAD_SIZE ** 0.5

    def one_block(block):
        starting_row = (block * QUERY_BLOCK_ROWS).astype(jnp.int32)
        query_row_block = lax.dynamic_slice_in_dim(query_vectors, starting_row, QUERY_BLOCK_ROWS, 0).astype(jnp.float32).reshape(QUERY_BLOCK_ROWS, KEY_VALUE_HEADS, HEADS_PER_GROUP, HEAD_SIZE)
        key_matrix_rows = lax.dynamic_slice_in_dim(padded_keys, starting_row, row_extent, 0).astype(jnp.float32).reshape(row_extent, KEY_VALUE_HEADS, HEAD_SIZE)
        value_matrix_rows = lax.dynamic_slice_in_dim(padded_values, starting_row, row_extent, 0).astype(jnp.float32).reshape(row_extent, KEY_VALUE_HEADS, HEAD_SIZE)
        key_pos = starting_row - MAXDOC + jnp.arange(row_extent, dtype=jnp.int32)
        query_pos = starting_row + jnp.arange(QUERY_BLOCK_ROWS, dtype=jnp.int32)
        row_first = lax.dynamic_slice_in_dim(first, starting_row, QUERY_BLOCK_ROWS, 0)
        allowed = (key_pos[None, :] >= row_first[:, None]) & (key_pos[None, :] <= query_pos[:, None])
        scores = jnp.einsum('qngd,knd->ngqk', query_row_block, key_matrix_rows) * scale
        scores = jnp.where(allowed, scores, -big_value)
        highest = lax.optimization_barrier(jnp.max(scores, axis=-1))
        weights = jnp.where(allowed, jnp.exp(scores - highest[..., None]), 0.0)
        total = lax.optimization_barrier(jnp.sum(weights, axis=-1))
        rounded = lax.optimization_barrier(weights.astype(jnp.bfloat16))
        summed = jnp.einsum('ngqk,knd->ngqd', rounded.astype(jnp.float32), value_matrix_rows)
        result = summed / total[..., None]
        result = jnp.transpose(result, (2, 0, 1, 3)).reshape(QUERY_BLOCK_ROWS, QUERY_HEADS * HEAD_SIZE).astype(jnp.bfloat16)
        lse = (highest + jnp.log(total)).reshape(QUERY_HEADS, QUERY_BLOCK_ROWS)
        return (result, lse)
    results, lses = lax.map(one_block, jnp.arange(NB, dtype=jnp.int32))
    attn_out = results.reshape(TOKENS, QUERY_HEADS * HEAD_SIZE)
    order = jnp.argsort(block_server * NB + jnp.arange(NB, dtype=jnp.int32), stable=True)
    served_lse = lses[order]
    return (attn_out, served_lse)
```

```python
import functools
import math

import jax
import jax.numpy as jnp
from jax import lax
from jax.experimental import pallas as pl
from jax.experimental.pallas import tpu as pltpu
from jax.sharding import PartitionSpec as P

HEAD_SIZE = 128
QUERY_BLOCK_ROWS = 128
CORES = 2

masked_value = -1e30
norm_eps = 1e-05
score_scale = 1.0 / HEAD_SIZE**0.5
log2_scale = score_scale * math.log2(math.e)

VMEM = pl.BlockSpec(memory_space=pltpu.VMEM)
SMEM = pl.BlockSpec(memory_space=pltpu.SMEM)
HBM = pl.BlockSpec(memory_space=pltpu.HBM)


def params(limit=16 << 20):
    return pltpu.CompilerParams(vmem_limit_bytes=limit)


def part_terms(x, gain):
    values = x.astype(jnp.float32)
    scaled = (values * gain).astype(jnp.bfloat16)
    return scaled, jnp.sum(values * values, axis=1, keepdims=True)


def cost():
    return pl.CostEstimate(flops=1 << 10, bytes_accessed=1 << 10, transcendentals=0)


class Weights:
    def __init__(self, order_ref, slots, features, hbm, vmem, sems):
        self.copies = {}
        for kind, (src, dst) in enumerate(zip(hbm, vmem)):
            for i, slot in enumerate(slots):
                start = pl.multiple_of(order_ref[slot] * features, features)
                rows = pl.ds(i * features, features)
                copy = pltpu.make_async_copy(
                    src.at[pl.ds(start, features), :], dst.at[rows, :], sems.at[kind, i]
                )
                copy.start()
                self.copies[kind, i] = copy
        self.vmem = vmem

    def product(self, scaled, kind):
        for (k, _), copy in self.copies.items():
            if k == kind:
                copy.wait()
        return jnp.dot(scaled, self.vmem[kind][...], preferred_element_type=jnp.float32)


def weight_scratch(count, features, weights):
    return [pltpu.VMEM((count * features, w.shape[1]), jnp.bfloat16) for w in weights] + [
        pltpu.SemaphoreType.DMA((len(weights), count))
    ]


def local_kernel(order_ref, docs_ref, x_ref, other_ref, gain_ref, wk, wv, wq, q_ref, kv_ref, sq_ref, bound_ref, *scratch):
    features = x_ref.shape[1]
    shape = bound_ref.shape
    base = order_ref[order_ref.shape[0] - 1]
    position = lax.broadcasted_iota(jnp.int32, shape, 0) * shape[1] + lax.broadcasted_iota(jnp.int32, shape, 1)
    start = -base
    bounds = jnp.full(shape, start, jnp.int32)
    for d in range(docs_ref.shape[0]):
        bounds = jnp.where(position >= start, start, bounds)
        start = start + docs_ref[d]
    bound_ref[...] = bounds
    width = wk.shape[1]
    weights = Weights(order_ref, range(CORES), features, (wk, wv, wq), scratch[:3], scratch[3])
    parts = [
        part_terms(ref[...], gain_ref[pl.ds(order_ref[slot], 1), :]) for slot, ref in enumerate((x_ref, other_ref))
    ]
    sq_ref[...] = parts[0][1] + parts[1][1]
    scaled = jnp.concatenate([part[0] for part in parts], axis=1)
    kv_ref[:, :width] = weights.product(scaled, 0)
    kv_ref[:, width:] = weights.product(scaled, 1)
    q_ref[...] = weights.product(scaled, 2)


def local_part(order, docs, x, other, gains, wk, wv, wq):
    rows, features = x.shape
    q_width, kv_width = wq.shape[1], 2 * wk.shape[1]
    return pl.pallas_call(
        local_kernel,
        out_shape=(
            jax.ShapeDtypeStruct((rows, q_width), jnp.float32),
            jax.ShapeDtypeStruct((rows, kv_width), jnp.float32),
            jax.ShapeDtypeStruct((rows, 1), jnp.float32),
            jax.ShapeDtypeStruct((rows // QUERY_BLOCK_ROWS, QUERY_BLOCK_ROWS), jnp.int32),
        ),
        in_specs=[SMEM, SMEM, VMEM, VMEM, VMEM, HBM, HBM, HBM],
        out_specs=(VMEM,) * 4,
        scratch_shapes=weight_scratch(CORES, features, (wk, wv, wq)),
        compiler_params=params(24 << 20),
        cost_estimate=cost(),
    )(order, docs, x, other, gains, wk, wv, wq)


def chunk_kernel(count, halves, row, want_kv, want_q, order_ref, *refs):
    it = iter(refs)
    groups = [[next(it) for _ in range(halves if i % CORES else 1)] for i in range(count)]
    gain_ref = next(it)
    hbm = [next(it) for _ in range(2 * want_kv + want_q)]
    kva_ref, sq_ref = (next(it), next(it)) if want_kv else (None, None)
    inv_ref = None if want_kv else next(it)
    qa_ref = next(it) if want_q else None
    kv_ref, inv_out = (next(it), next(it)) if want_kv else (None, None)
    q_ref = next(it) if want_q else None
    *vmem, sems = it
    features = groups[0][0].shape[1]
    weights = Weights(order_ref, [CORES + i for i in range(count)], features, hbm, vmem, sems)
    scaled, squares = [], []
    for i, group in enumerate(groups):
        x = jnp.concatenate([ref[...] for ref in group], axis=0)
        part, square = part_terms(x, gain_ref[pl.ds(order_ref[CORES + i], 1), :])
        scaled.append(part)
        squares.append(square)
    scaled = jnp.concatenate(scaled, axis=1)
    rows = scaled.shape[0]
    here = slice(row, row + rows)
    if want_kv:
        width = hbm[0].shape[1]
        inverse = lax.rsqrt((sq_ref[here, :] + sum(squares)) / (features * (count + CORES)) + norm_eps)
        inv_out[...] = inverse
        for kind in range(2):
            columns = slice(kind * width, (kind + 1) * width)
            total = kva_ref[here, columns] + weights.product(scaled, kind)
            kv_ref[:, columns] = (total * inverse).astype(jnp.bfloat16)
    else:
        inverse = inv_ref[...]
    if want_q:
        total = qa_ref[here, :] + weights.product(scaled, len(hbm) - 1)
        q_ref[...] = (total * inverse).astype(jnp.bfloat16)


def project(row, order, groups, gains, wk=None, wv=None, wq=None, kv_acc=None, squares=None, inverse=None, q_acc=None):
    want_kv, want_q = wk is not None, wq is not None
    count, (rows, features) = len(groups), groups[0][0].shape
    weights = ([wk, wv] if want_kv else []) + ([wq] if want_q else [])
    pieces = [piece for group in groups for piece in group]
    accs = ([kv_acc, squares] if want_kv else [inverse]) + ([q_acc] if want_q else [])
    shapes = []
    if want_kv:
        shapes += [jax.ShapeDtypeStruct((rows, 2 * wk.shape[1]), jnp.bfloat16), jax.ShapeDtypeStruct((rows, 1), jnp.float32)]
    if want_q:
        shapes += [jax.ShapeDtypeStruct((rows, wq.shape[1]), jnp.bfloat16)]
    return pl.pallas_call(
        functools.partial(chunk_kernel, count, len(groups[1]), row, want_kv, want_q),
        out_shape=tuple(shapes),
        in_specs=[SMEM] + [VMEM] * (len(pieces) + 1) + [HBM] * len(weights) + [VMEM] * len(accs),
        out_specs=(VMEM,) * len(shapes),
        scratch_shapes=weight_scratch(count, features, weights),
        compiler_params=params(24 << 20),
        cost_estimate=cost(),
    )(order, *pieces, gains, *weights, *accs)


def block_attention(q, bounds, keys_values, key_starts, row_start, store):
    rows = q.shape[0]
    width = keys_values[0].shape[1] // 2
    kv_heads = width // HEAD_SIZE
    group = q.shape[1] // width
    bounds = jnp.transpose(jnp.broadcast_to(bounds, (QUERY_BLOCK_ROWS, rows)))
    query_pos = row_start + lax.broadcasted_iota(jnp.int32, (rows, QUERY_BLOCK_ROWS), 0)
    allowed = []
    for start in key_starts:
        key_pos = start + lax.broadcasted_iota(jnp.int32, (rows, QUERY_BLOCK_ROWS), 1)
        ok = key_pos >= bounds
        if start == row_start:
            ok = ok & (key_pos <= query_pos)
        allowed.append(jnp.concatenate([ok] * group, axis=0))
    lse_rows = []
    for n in range(kv_heads):
        stacked = jnp.concatenate(
            [q[:, (n * group + g) * HEAD_SIZE : (n * group + g + 1) * HEAD_SIZE] for g in range(group)],
            axis=0,
        )
        scores = []
        highest = None
        for ok, ref in zip(allowed, keys_values):
            s = lax.dot_general(
                stacked,
                ref[:, n * HEAD_SIZE : (n + 1) * HEAD_SIZE],
                (((1,), (1,)), ((), ())),
                preferred_element_type=jnp.float32,
            )
            s = jnp.where(ok, s, masked_value)
            scores.append(s)
            highest = s if highest is None else jnp.maximum(highest, s)
        highest = jnp.max(highest, axis=1, keepdims=True)
        total = None
        summed = None
        for s, ref in zip(scores, keys_values):
            weights = jnp.exp2((s - highest) * log2_scale)
            total = weights if total is None else total + weights
            product = jnp.dot(
                weights.astype(jnp.bfloat16),
                ref[:, width + n * HEAD_SIZE : width + (n + 1) * HEAD_SIZE],
                preferred_element_type=jnp.float32,
            )
            summed = product if summed is None else summed + product
        total = jnp.sum(total, axis=1, keepdims=True)
        result = (summed / total).astype(jnp.bfloat16)
        lse = highest * score_scale + jnp.log(total)
        for g in range(group):
            store(n * group + g, result[g * rows : (g + 1) * rows])
            lse_rows.append(lse[g * rows : (g + 1) * rows])
    lane = lax.broadcasted_iota(jnp.int32, (rows, HEAD_SIZE), 1)
    table = jnp.zeros((rows, HEAD_SIZE), jnp.float32)
    for h, column in enumerate(lse_rows):
        table = jnp.where(lane == h, column, table)
    return jnp.transpose(table)[: len(lse_rows), :]


def main_attention_kernel(blocks, *refs):
    qs, owns, priors = refs[: blocks - 1], refs[blocks - 1 : 2 * blocks - 1], refs[2 * blocks - 1 : 3 * blocks - 2]
    bounds_ref, out_ref, lse_ref = refs[3 * blocks - 2 :]
    rows = QUERY_BLOCK_ROWS
    for block in range(1, blocks):
        def store(head, value, block=block):
            out_ref[block * rows : (block + 1) * rows, head * HEAD_SIZE : (head + 1) * HEAD_SIZE] = value

        lse_ref[block - 1] = block_attention(
            qs[block - 1][...],
            bounds_ref[block : block + 1, :],
            [*priors[block - 1 :], *owns[: block + 1]],
            [(i - blocks) * rows for i in range(block, blocks)] + [i * rows for i in range(block + 1)],
            block * rows,
            store,
        )


def last_attention_kernel(blocks, servers, *refs):
    server_ref, q_ref, own_ref = refs[:3]
    priors = refs[3 : 3 + blocks]
    bounds_ref, lse_ref, _, out_ref, send_ref = refs[3 + blocks :]
    rows = QUERY_BLOCK_ROWS

    def store(head, value):
        out_ref[:, head * HEAD_SIZE : (head + 1) * HEAD_SIZE] = value

    lses = [
        block_attention(
            q_ref[...],
            bounds_ref[:1, :],
            [*priors, own_ref],
            [(i - blocks) * rows for i in range(blocks)] + [0],
            0,
            store,
        )
    ]
    lses += [lse_ref[i] for i in range(blocks - 1)]
    for s in range(servers):
        value = jnp.full(lses[0].shape, jnp.inf, jnp.float32)
        for i in range(blocks):
            value = jnp.where(server_ref[i] == s, lses[i], value)
        send_ref[s] = value.astype(jnp.bfloat16)


def pick_kernel(blocks, recv_ref, out_ref):
    shape = recv_ref.shape[1:]
    rank = jnp.zeros(shape, jnp.int32)
    picked = [jnp.zeros(shape, jnp.float32) for _ in range(blocks)]
    for i in range(recv_ref.shape[0]):
        value = recv_ref[i].astype(jnp.float32)
        valid = value < jnp.inf
        for k in range(blocks):
            picked[k] = jnp.where(valid & (rank == k), value, picked[k])
        rank = rank + valid.astype(jnp.int32)
    for k in range(blocks):
        out_ref[k] = picked[k]


def shards(tokens, norm_gain, w_query, w_key, value_matrix, doc_lengths, block_server):
    rows, features = tokens.shape
    width = w_key.shape[1]
    heads = w_query.shape[1] // HEAD_SIZE
    block = QUERY_BLOCK_ROWS
    blocks = rows // block
    servers = lax.axis_size("attn")
    sharers = lax.axis_size("proj")
    chips = sharers // CORES
    me_attn = lax.axis_index("attn")
    me_proj = lax.axis_index("proj")
    sibling = [(i, i ^ 1) for i in range(sharers)]

    def across(distance):
        return [(i, (i + distance * CORES) % sharers) for i in range(sharers)]

    chunks = list(range(blocks))[::-1]
    arrived = {}
    rest = tokens
    for c in chunks:
        piece = rest[c * block : (c + 1) * block]
        if c == chunks[0]:
            piece, rest = lax.optimization_barrier((piece, rest))
        arrived[c] = [lax.ppermute(piece, "proj", across(d)) for d in range(1, chips)]
    other = lax.ppermute(tokens, "proj", sibling)

    order = [me_proj, me_proj ^ 1]
    for d in range(1, chips):
        source = (me_proj + sharers - d * CORES) % sharers
        order += [source, source ^ 1]
    order = jnp.stack([*order, me_attn * rows]).astype(jnp.int32)
    gains = norm_gain.reshape(sharers, features)

    w_key, value_matrix, w_query = [
        pltpu.with_memory_space_constraint(w, pltpu.HBM) for w in (w_key, value_matrix, w_query)
    ]
    q_acc, kv_acc, squares, bounds = local_part(
        order, doc_lengths, tokens, other, gains, w_key, value_matrix, w_query
    )

    onward = [(i, (i + 1) % servers) for i in range(servers)]
    own, prior, queries = [None] * blocks, [None] * blocks, [None] * blocks
    tie = kv_acc
    halves = 2
    for c in chunks:
        pieces, tie = lax.optimization_barrier((arrived[c], tie))
        groups = []
        for piece in pieces:
            part = block // halves
            groups += [
                [piece],
                [lax.ppermute(piece[i * part : (i + 1) * part], "proj", sibling) for i in range(halves)],
            ]
        if c:
            own[c], inverse, queries[c] = project(
                c * block, order, groups, gains, w_key, value_matrix, w_query, kv_acc, squares, None, q_acc
            )
            prior[c] = lax.ppermute(own[c], "attn", onward)
        else:
            own[c], inverse = project(c * block, order, groups, gains, w_key, value_matrix, None, kv_acc, squares)
            prior[c] = lax.ppermute(own[c], "attn", onward)
            (queries[c],) = project(c * block, order, groups, gains, None, None, w_query, None, None, inverse, q_acc)
        tie = (queries[c], prior[c + 1]) if c + 1 < blocks else queries[c]

    out, lse = pl.pallas_call(
        functools.partial(main_attention_kernel, blocks),
        out_shape=(
            jax.ShapeDtypeStruct((rows, heads * HEAD_SIZE), jnp.bfloat16),
            jax.ShapeDtypeStruct((blocks - 1, heads, block), jnp.float32),
        ),
        in_specs=[VMEM] * (3 * blocks - 1),
        out_specs=(VMEM, VMEM),
        compiler_params=params(24 << 20),
        cost_estimate=cost(),
    )(*queries[1:], *own, *prior[1:], bounds)
    out, send = pl.pallas_call(
        functools.partial(last_attention_kernel, blocks, servers),
        grid=(1,),
        out_shape=(
            jax.ShapeDtypeStruct((rows, heads * HEAD_SIZE), jnp.bfloat16),
            jax.ShapeDtypeStruct((servers, heads, block), jnp.bfloat16),
        ),
        in_specs=[SMEM] + [VMEM] * (blocks + 4) + [pl.BlockSpec(memory_space=pl.ANY)],
        out_specs=(pl.BlockSpec((block, heads * HEAD_SIZE), lambda i: (0, 0)), VMEM),
        input_output_aliases={blocks + 5: 0},
        compiler_params=params(),
        cost_estimate=cost(),
    )(block_server, queries[0], own[0], *prior, bounds, lse, out)
    recv = lax.all_to_all(send, "attn", split_axis=0, concat_axis=0, tiled=True)
    served = pl.pallas_call(
        functools.partial(pick_kernel, blocks),
        out_shape=jax.ShapeDtypeStruct((blocks, heads, block), jnp.float32),
        in_specs=[VMEM],
        out_specs=VMEM,
        compiler_params=params(),
    )(recv)
    return (out, served)


def solution(mesh):
    return jax.shard_map(
        shards,
        mesh=mesh,
        in_specs=(
            P("attn", "proj"),
            P(),
            P(None, "proj"),
            P(None, "proj"),
            P(None, "proj"),
            P(),
            P("attn"),
        ),
        out_specs=(P("attn", "proj"), P("attn", "proj", None)),
        check_vma=False,
    )
```

```python
import functools
import math

import jax
import jax.numpy as jnp
from jax import lax
from jax.experimental import pallas as pl
from jax.experimental.pallas import tpu as pltpu
from jax.sharding import PartitionSpec as P

HEAD_SIZE = 128
QUERY_BLOCK_ROWS = 128
CORES = 2

masked_value = -1e30
norm_eps = 1e-05
score_scale = 1.0 / HEAD_SIZE**0.5
log2_scale = score_scale * math.log2(math.e)

VMEM = pl.BlockSpec(memory_space=pltpu.VMEM)
SMEM = pl.BlockSpec(memory_space=pltpu.SMEM)
HBM = pl.BlockSpec(memory_space=pltpu.HBM)


def params(limit=16 << 20):
    return pltpu.CompilerParams(vmem_limit_bytes=limit)


def part_terms(x, gain):
    values = x.astype(jnp.float32)
    scaled = (values * gain).astype(jnp.bfloat16)
    return scaled, jnp.sum(values * values, axis=1, keepdims=True)


def cost():
    return pl.CostEstimate(flops=1 << 10, bytes_accessed=1 << 10, transcendentals=0)


def local_kernel(order_ref, docs_ref, x_ref, other_ref, gain_ref, wk, wv, wq, *refs):
    q_ref, kv_ref, sq_ref, bound_ref, kv_rest, q_rest, kv_own, q_own, sems = refs
    features, width = x_ref.shape[1], wk.shape[1]

    def fetch(slot, kv_to, q_to, place):
        rows = pl.ds(pl.multiple_of(order_ref[slot] * features, features), features)
        here = pl.ds(place * features, features)
        copies = (
            pltpu.make_async_copy(wk.at[rows, :], kv_to.at[here, pl.ds(0, width)], sems.at[slot, 0]),
            pltpu.make_async_copy(wv.at[rows, :], kv_to.at[here, pl.ds(width, width)], sems.at[slot, 1]),
            pltpu.make_async_copy(wq.at[rows, :], q_to.at[here, :], sems.at[slot, 2]),
        )
        for copy in copies:
            copy.start()
        return copies

    mine = [fetch(slot, kv_own, q_own, slot) for slot in range(CORES)]
    rest = [fetch(CORES + i, kv_rest, q_rest, i) for i in range(q_rest.shape[0] // features)]

    shape = bound_ref.shape
    base = order_ref[order_ref.shape[0] - 1]
    position = lax.broadcasted_iota(jnp.int32, shape, 0) * shape[1] + lax.broadcasted_iota(jnp.int32, shape, 1)
    start = -base
    bounds = jnp.full(shape, start, jnp.int32)
    for d in range(docs_ref.shape[0]):
        bounds = jnp.where(position >= start, start, bounds)
        start = start + docs_ref[d]
    bound_ref[...] = bounds

    parts = [
        part_terms(ref[...], gain_ref[pl.ds(order_ref[slot], 1), :]) for slot, ref in enumerate((x_ref, other_ref))
    ]
    sq_ref[...] = parts[0][1] + parts[1][1]
    scaled = jnp.concatenate([part[0] for part in parts], axis=1)
    for k, v, _ in mine:
        k.wait()
        v.wait()
    kv_ref[...] = jnp.dot(scaled, kv_own[...], preferred_element_type=jnp.float32)
    for _, _, q in mine:
        q.wait()
    q_ref[...] = jnp.dot(scaled, q_own[...], preferred_element_type=jnp.float32)
    for copies in rest:
        for copy in copies:
            copy.wait()


def local_part(order, docs, x, other, gains, wk, wv, wq):
    rows, features = x.shape
    q_width, kv_width = wq.shape[1], 2 * wk.shape[1]
    rest = wq.shape[0] - CORES * features
    return pl.pallas_call(
        local_kernel,
        out_shape=(
            pltpu.VMEM((rows, q_width), jnp.float32),
            pltpu.VMEM((rows, kv_width), jnp.float32),
            pltpu.VMEM((rows, 1), jnp.float32),
            pltpu.VMEM((rows // QUERY_BLOCK_ROWS, QUERY_BLOCK_ROWS), jnp.int32),
            pltpu.VMEM((rest, kv_width), jnp.bfloat16),
            pltpu.VMEM((rest, q_width), jnp.bfloat16),
        ),
        in_specs=[SMEM, SMEM, VMEM, VMEM, VMEM, HBM, HBM, HBM],
        out_specs=(VMEM,) * 6,
        scratch_shapes=[
            pltpu.VMEM((CORES * features, kv_width), jnp.bfloat16),
            pltpu.VMEM((CORES * features, q_width), jnp.bfloat16),
            pltpu.SemaphoreType.DMA((wq.shape[0] // features, 3)),
        ],
        compiler_params=params(32 << 20),
        cost_estimate=cost(),
    )(order, docs, x, other, gains, wk, wv, wq)


def chunk_kernel(count, halves, row, want_kv, want_q, order_ref, *refs):
    it = iter(refs)
    groups = [[next(it) for _ in range(halves if i % CORES else 1)] for i in range(count)]
    gain_ref = next(it)
    wkv_ref, kva_ref, sq_ref = (next(it), next(it), next(it)) if want_kv else (None,) * 3
    inv_ref = None if want_kv else next(it)
    wq_ref, qa_ref = (next(it), next(it)) if want_q else (None, None)
    kv_ref, inv_out = (next(it), next(it)) if want_kv else (None, None)
    q_ref = next(it) if want_q else None
    features = groups[0][0].shape[1]
    scaled, squares = [], []
    for i, group in enumerate(groups):
        x = jnp.concatenate([ref[...] for ref in group], axis=0)
        part, square = part_terms(x, gain_ref[pl.ds(order_ref[CORES + i], 1), :])
        scaled.append(part)
        squares.append(square)
    scaled = jnp.concatenate(scaled, axis=1)
    here = slice(row, row + scaled.shape[0])
    if want_kv:
        inverse = lax.rsqrt((sq_ref[here, :] + sum(squares)) / (features * (count + CORES)) + norm_eps)
        inv_out[...] = inverse
        total = kva_ref[here, :] + jnp.dot(scaled, wkv_ref[...], preferred_element_type=jnp.float32)
        kv_ref[...] = (total * inverse).astype(jnp.bfloat16)
    else:
        inverse = inv_ref[...]
    if want_q:
        total = qa_ref[here, :] + jnp.dot(scaled, wq_ref[...], preferred_element_type=jnp.float32)
        q_ref[...] = (total * inverse).astype(jnp.bfloat16)


def project(row, order, groups, gains, kv=(), inverse=None, q=()):
    count, halves, rows = len(groups), len(groups[1]), groups[0][0].shape[0]
    pieces = [piece for group in groups for piece in group]
    operands = [*kv] + ([] if kv else [inverse]) + [*q]
    shapes = []
    if kv:
        shapes += [
            jax.ShapeDtypeStruct((rows, kv[0].shape[1]), jnp.bfloat16),
            jax.ShapeDtypeStruct((rows, 1), jnp.float32),
        ]
    if q:
        shapes += [jax.ShapeDtypeStruct((rows, q[0].shape[1]), jnp.bfloat16)]
    return pl.pallas_call(
        functools.partial(chunk_kernel, count, halves, row, bool(kv), bool(q)),
        out_shape=tuple(shapes),
        in_specs=[SMEM] + [VMEM] * (len(pieces) + 1 + len(operands)),
        out_specs=(VMEM,) * len(shapes),
        compiler_params=params(),
        cost_estimate=cost(),
    )(order, *pieces, gains, *operands)


def block_attention(q, bounds, keys_values, key_starts, row_start, store):
    rows = q.shape[0]
    width = keys_values[0][0].shape[1] // 2
    kv_heads = width // HEAD_SIZE
    group = q.shape[1] // width
    bounds = jnp.transpose(jnp.broadcast_to(bounds, (QUERY_BLOCK_ROWS, rows)))
    query_pos = row_start + lax.broadcasted_iota(jnp.int32, (rows, QUERY_BLOCK_ROWS), 0)
    allowed = []
    for start in key_starts:
        key_pos = start + lax.broadcasted_iota(jnp.int32, (rows, QUERY_BLOCK_ROWS), 1)
        ok = key_pos >= bounds
        if start == row_start:
            ok = ok & (key_pos <= query_pos)
        allowed.append(jnp.concatenate([ok] * group, axis=0))
    lse_rows = []
    for n in range(kv_heads):
        stacked = jnp.concatenate(
            [q[:, (n * group + g) * HEAD_SIZE : (n * group + g + 1) * HEAD_SIZE] for g in range(group)],
            axis=0,
        )
        scores = []
        highest = None
        for ok, (ref, at) in zip(allowed, keys_values):
            s = lax.dot_general(
                stacked,
                ref[at : at + QUERY_BLOCK_ROWS, n * HEAD_SIZE : (n + 1) * HEAD_SIZE],
                (((1,), (1,)), ((), ())),
                preferred_element_type=jnp.float32,
            )
            s = jnp.where(ok, s, masked_value)
            scores.append(s)
            highest = s if highest is None else jnp.maximum(highest, s)
        highest = jnp.max(highest, axis=1, keepdims=True)
        total = None
        summed = None
        for s, (ref, at) in zip(scores, keys_values):
            weights = jnp.exp2((s - highest) * log2_scale)
            total = weights if total is None else total + weights
            product = jnp.dot(
                weights.astype(jnp.bfloat16),
                ref[at : at + QUERY_BLOCK_ROWS, width + n * HEAD_SIZE : width + (n + 1) * HEAD_SIZE],
                preferred_element_type=jnp.float32,
            )
            summed = product if summed is None else summed + product
        total = jnp.sum(total, axis=1, keepdims=True)
        result = (summed / total).astype(jnp.bfloat16)
        lse = highest * score_scale + jnp.log(total)
        for g in range(group):
            store(n * group + g, result[g * rows : (g + 1) * rows])
            lse_rows.append(lse[g * rows : (g + 1) * rows])
    lane = lax.broadcasted_iota(jnp.int32, (rows, HEAD_SIZE), 1)
    table = jnp.zeros((rows, HEAD_SIZE), jnp.float32)
    for h, column in enumerate(lse_rows):
        table = jnp.where(lane == h, column, table)
    return jnp.transpose(table)[: len(lse_rows), :]


def block_refs(refs, chunks):
    found = {}
    for ref, (low, high) in zip(refs, chunks):
        for i in range(low, high):
            found[i] = (ref, (i - low) * QUERY_BLOCK_ROWS)
    return found


def attend_blocks(wanted, blocks, queries, owns, priors, bounds_ref, out_ref, base):
    rows = QUERY_BLOCK_ROWS
    lses = {}
    for block in wanted:
        def store(head, value, at=(block - base) * rows):
            out_ref[at : at + rows, head * HEAD_SIZE : (head + 1) * HEAD_SIZE] = value

        ref, at = queries[block]
        lses[block] = block_attention(
            ref[at : at + rows, :],
            bounds_ref[block : block + 1, :],
            [priors[i] for i in range(block, blocks)] + [owns[i] for i in range(block + 1)],
            [(i - blocks) * rows for i in range(block, blocks)] + [i * rows for i in range(block + 1)],
            block * rows,
            store,
        )
    return lses


def main_attention_kernel(chunks, *refs):
    count, (low, blocks) = len(chunks), chunks[0]
    queries = block_refs(refs[:1], chunks[:1])
    owns = block_refs(refs[1 : 1 + count], chunks)
    priors = block_refs(refs[1 + count : 2 + count], chunks[:1])
    bounds_ref, out_ref, lse_ref = refs[2 + count :]
    lses = attend_blocks(range(low, blocks), blocks, queries, owns, priors, bounds_ref, out_ref, low)
    for block, lse in lses.items():
        lse_ref[block - low] = lse


def last_attention_kernel(chunks, servers, *refs):
    count, (low, blocks) = len(chunks), chunks[0]
    server_ref, *refs = refs
    queries = block_refs(refs[: count - 1], chunks[1:])
    owns = block_refs(refs[count - 1 : 2 * count - 2], chunks[1:])
    priors = block_refs(refs[2 * count - 2 : 3 * count - 2], chunks)
    bounds_ref, lse_ref, _, out_ref, send_ref = refs[3 * count - 2 :]
    lses = attend_blocks(reversed(range(low)), blocks, queries, owns, priors, bounds_ref, out_ref, 0)
    for block in range(low, blocks):
        lses[block] = lse_ref[block - low]
    for s in range(servers):
        value = jnp.full(lses[0].shape, jnp.inf, jnp.float32)
        for block, lse in lses.items():
            value = jnp.where(server_ref[block] == s, lse, value)
        send_ref[s] = value.astype(jnp.bfloat16)


def pick_kernel(blocks, recv_ref, out_ref):
    shape = recv_ref.shape[1:]
    rank = jnp.zeros(shape, jnp.int32)
    picked = [jnp.zeros(shape, jnp.float32) for _ in range(blocks)]
    for i in range(recv_ref.shape[0]):
        value = recv_ref[i].astype(jnp.float32)
        valid = value < jnp.inf
        for k in range(blocks):
            picked[k] = jnp.where(valid & (rank == k), value, picked[k])
        rank = rank + valid.astype(jnp.int32)
    for k in range(blocks):
        out_ref[k] = picked[k]


def shards(tokens, norm_gain, w_query, w_key, value_matrix, doc_lengths, block_server):
    rows, features = tokens.shape
    width = w_key.shape[1]
    heads = w_query.shape[1] // HEAD_SIZE
    block = QUERY_BLOCK_ROWS
    blocks = rows // block
    servers = lax.axis_size("attn")
    sharers = lax.axis_size("proj")
    chips = sharers // CORES
    me_attn = lax.axis_index("attn")
    me_proj = lax.axis_index("proj")
    sibling = [(i, i ^ 1) for i in range(sharers)]

    def across(distance):
        return [(i, (i + distance * CORES) % sharers) for i in range(sharers)]

    middle = blocks // 2
    chunks = [(middle, blocks)] + [(i, i + 1) for i in reversed(range(middle))]
    arrived = []
    rest = tokens
    for low, high in chunks:
        piece = rest[low * block : high * block]
        if not arrived:
            piece, rest = lax.optimization_barrier((piece, rest))
        arrived.append([lax.ppermute(piece, "proj", across(d)) for d in range(1, chips)])
    other = lax.ppermute(tokens, "proj", sibling)

    order = [me_proj, me_proj ^ 1]
    for d in range(1, chips):
        source = (me_proj + sharers - d * CORES) % sharers
        order += [source, source ^ 1]
    order = jnp.stack([*order, me_attn * rows]).astype(jnp.int32)
    gains = norm_gain.reshape(sharers, features)

    w_key, value_matrix, w_query = [
        pltpu.with_memory_space_constraint(w, pltpu.HBM) for w in (w_key, value_matrix, w_query)
    ]
    q_acc, kv_acc, squares, bounds, wkv_rest, wq_rest = local_part(
        order, doc_lengths, tokens, other, gains, w_key, value_matrix, w_query
    )

    onward = [(i, (i + 1) % servers) for i in range(servers)]
    own, prior, queries = [], [], []
    tie = kv_acc
    for (low, high), pieces in zip(chunks, arrived):
        pieces, tie = lax.optimization_barrier((pieces, tie))
        part = 64 if high == blocks else 32
        groups = []
        for piece in pieces:
            groups += [
                [piece],
                [lax.ppermute(piece[i : i + part], "proj", sibling) for i in range(0, piece.shape[0], part)],
            ]
        if low:
            kv, _, q = project(
                low * block, order, groups, gains, (wkv_rest, kv_acc, squares), None, (wq_rest, q_acc)
            )
            tie = q
            prior.append(lax.ppermute(kv, "attn", onward))
        else:
            kv, inverse = project(0, order, groups, gains, (wkv_rest, kv_acc, squares))
            prior.append(lax.ppermute(kv, "attn", onward))
            (q,) = project(0, order, groups, gains, (), inverse, (wq_rest, q_acc))
        own.append(kv)
        queries.append(q)

    count = len(chunks)
    queries = list(lax.optimization_barrier(tuple(queries)))
    half = (blocks - middle) * block
    out, lse = pl.pallas_call(
        functools.partial(main_attention_kernel, chunks),
        grid=(1,),
        out_shape=(
            jax.ShapeDtypeStruct((rows, heads * HEAD_SIZE), jnp.bfloat16),
            jax.ShapeDtypeStruct((blocks - middle, heads, block), jnp.float32),
        ),
        in_specs=[VMEM] * (count + 3),
        out_specs=(pl.BlockSpec((half, heads * HEAD_SIZE), lambda i: (rows // half - 1, 0)), VMEM),
        compiler_params=params(24 << 20),
        cost_estimate=cost(),
    )(queries[0], *own, prior[0], bounds)
    out, send = pl.pallas_call(
        functools.partial(last_attention_kernel, chunks, servers),
        grid=(1,),
        out_shape=(
            jax.ShapeDtypeStruct((rows, heads * HEAD_SIZE), jnp.bfloat16),
            jax.ShapeDtypeStruct((servers, heads, block), jnp.bfloat16),
        ),
        in_specs=[SMEM] + [VMEM] * (3 * count) + [pl.BlockSpec(memory_space=pl.ANY)],
        out_specs=(pl.BlockSpec((rows - half, heads * HEAD_SIZE), lambda i: (0, 0)), VMEM),
        input_output_aliases={3 * count + 1: 0},
        compiler_params=params(24 << 20),
        cost_estimate=cost(),
    )(block_server, *queries[1:], *own[1:], *prior, bounds, lse, out)
    recv = lax.all_to_all(send, "attn", split_axis=0, concat_axis=0, tiled=True)
    served = pl.pallas_call(
        functools.partial(pick_kernel, blocks),
        out_shape=jax.ShapeDtypeStruct((blocks, heads, block), jnp.float32),
        in_specs=[VMEM],
        out_specs=VMEM,
        compiler_params=params(),
    )(recv)
    return (out, served)


def solution(mesh):
    return jax.shard_map(
        shards,
        mesh=mesh,
        in_specs=(
            P("attn", "proj"),
            P(),
            P(None, "proj"),
            P(None, "proj"),
            P(None, "proj"),
            P(),
            P("attn"),
        ),
        out_specs=(P("attn", "proj"), P("attn", "proj", None)),
        check_vma=False,
    )
```

```python
import functools
import math

import jax
import jax.numpy as jnp
from jax import lax
from jax.experimental import pallas as pl
from jax.experimental.pallas import tpu as pltpu
from jax.sharding import PartitionSpec as P

HEAD_SIZE = 128
QUERY_BLOCK_ROWS = 128
CORES = 2
LAST_ROWS = 128

masked_value = -1e30
norm_eps = 1e-05
score_scale = 1.0 / HEAD_SIZE**0.5
log2_scale = score_scale * math.log2(math.e)

VMEM = pl.BlockSpec(memory_space=pltpu.VMEM)
SMEM = pl.BlockSpec(memory_space=pltpu.SMEM)
HBM = pl.BlockSpec(memory_space=pltpu.HBM)


def params(limit=16 << 20):
    return pltpu.CompilerParams(vmem_limit_bytes=limit)


def part_terms(x, gain):
    values = x.astype(jnp.float32)
    scaled = (values * gain).astype(jnp.bfloat16)
    return scaled, jnp.sum(values * values, axis=1, keepdims=True)


def cost():
    return pl.CostEstimate(flops=1 << 10, bytes_accessed=1 << 10, transcendentals=0)


def local_kernel(order_ref, docs_ref, x_ref, other_ref, gain_ref, wk, wv, wq, *refs):
    q_ref, kv_ref, sq_ref, bound_ref, kv_rest, q_rest, kv_own, q_own, sems = refs
    features, width = x_ref.shape[1], wk.shape[1]

    def fetch(slot, kv_to, q_to, place):
        rows = pl.ds(pl.multiple_of(order_ref[slot] * features, features), features)
        here = pl.ds(place * features, features)
        copies = (
            pltpu.make_async_copy(wk.at[rows, :], kv_to.at[here, pl.ds(0, width)], sems.at[slot, 0]),
            pltpu.make_async_copy(wv.at[rows, :], kv_to.at[here, pl.ds(width, width)], sems.at[slot, 1]),
            pltpu.make_async_copy(wq.at[rows, :], q_to.at[here, :], sems.at[slot, 2]),
        )
        for copy in copies:
            copy.start()
        return copies

    mine = [fetch(slot, kv_own, q_own, slot) for slot in range(CORES)]
    rest = [fetch(CORES + i, kv_rest, q_rest, i) for i in range(q_rest.shape[0] // features)]

    shape = bound_ref.shape
    base = order_ref[order_ref.shape[0] - 1]
    position = lax.broadcasted_iota(jnp.int32, shape, 0) * shape[1] + lax.broadcasted_iota(jnp.int32, shape, 1)
    start = -base
    bounds = jnp.full(shape, start, jnp.int32)
    for d in range(docs_ref.shape[0]):
        bounds = jnp.where(position >= start, start, bounds)
        start = start + docs_ref[d]
    bound_ref[...] = bounds

    parts = [
        part_terms(ref[...], gain_ref[pl.ds(order_ref[slot], 1), :]) for slot, ref in enumerate((x_ref, other_ref))
    ]
    sq_ref[...] = parts[0][1] + parts[1][1]
    scaled = jnp.concatenate([part[0] for part in parts], axis=1)
    for k, v, _ in mine:
        k.wait()
        v.wait()
    kv_ref[...] = jnp.dot(scaled, kv_own[...], preferred_element_type=jnp.float32)
    for _, _, q in mine:
        q.wait()
    q_ref[...] = jnp.dot(scaled, q_own[...], preferred_element_type=jnp.float32)
    for copies in rest:
        for copy in copies:
            copy.wait()


def local_part(order, docs, x, other, gains, wk, wv, wq):
    rows, features = x.shape
    q_width, kv_width = wq.shape[1], 2 * wk.shape[1]
    rest = wq.shape[0] - CORES * features
    return pl.pallas_call(
        local_kernel,
        out_shape=(
            pltpu.VMEM((rows, q_width), jnp.float32),
            pltpu.VMEM((rows, kv_width), jnp.float32),
            pltpu.VMEM((rows, 1), jnp.float32),
            pltpu.VMEM((rows // QUERY_BLOCK_ROWS, QUERY_BLOCK_ROWS), jnp.int32),
            pltpu.VMEM((rest, kv_width), jnp.bfloat16),
            pltpu.VMEM((rest, q_width), jnp.bfloat16),
        ),
        in_specs=[SMEM, SMEM, VMEM, VMEM, VMEM, HBM, HBM, HBM],
        out_specs=(VMEM,) * 6,
        scratch_shapes=[
            pltpu.VMEM((CORES * features, kv_width), jnp.bfloat16),
            pltpu.VMEM((CORES * features, q_width), jnp.bfloat16),
            pltpu.SemaphoreType.DMA((wq.shape[0] // features, 3)),
        ],
        compiler_params=params(32 << 20),
        cost_estimate=cost(),
    )(order, docs, x, other, gains, wk, wv, wq)


def chunk_kernel(sizes, row, order_ref, *refs):
    pieces, refs = refs[: sum(sizes)], refs[sum(sizes) :]
    gain_ref, wkv_ref, kva_ref, sq_ref, wq_ref, qa_ref, kv_ref, q_ref = refs
    terms = []
    for i, size in enumerate(sizes):
        x = jnp.concatenate([ref[...] for ref in pieces[:size]], axis=0)
        pieces = pieces[size:]
        terms.append(part_terms(x, gain_ref[pl.ds(order_ref[CORES + i], 1), :]))
    scaled = jnp.concatenate([x for x, _ in terms], axis=1)
    squares = sum(square for _, square in terms)
    here = slice(row, row + scaled.shape[0])
    features = scaled.shape[1] // len(sizes)
    inverse = lax.rsqrt((sq_ref[here, :] + squares) / (features * (len(sizes) + CORES)) + norm_eps)
    total = kva_ref[here, :] + jnp.dot(scaled, wkv_ref[...], preferred_element_type=jnp.float32)
    kv_ref[...] = (total * inverse).astype(jnp.bfloat16)
    total = qa_ref[here, :] + jnp.dot(scaled, wq_ref[...], preferred_element_type=jnp.float32)
    q_ref[...] = (total * (inverse * log2_scale)).astype(jnp.bfloat16)


def project(rows, row, order, groups, gains, wkv, kv_acc, squares, wq, q_acc):
    operands = [piece for group in groups for piece in group] + [gains, wkv, kv_acc, squares, wq, q_acc]
    return pl.pallas_call(
        functools.partial(chunk_kernel, [len(group) for group in groups], row),
        out_shape=(
            jax.ShapeDtypeStruct((rows, wkv.shape[1]), jnp.bfloat16),
            jax.ShapeDtypeStruct((rows, wq.shape[1]), jnp.bfloat16),
        ),
        in_specs=[SMEM] + [VMEM] * len(operands),
        out_specs=(VMEM, VMEM),
        compiler_params=params(),
        cost_estimate=cost(),
    )(order, *operands)


def block_parts(refs, chunks):
    found = {}
    block = QUERY_BLOCK_ROWS
    for i in range(chunks[0][1] // block):
        parts = []
        for ref, (low, high) in zip(refs, chunks):
            first, last = max(low, i * block), min(high, (i + 1) * block)
            if first < last:
                parts.insert(0, (ref, first - low, last - low))
        if sum(last - first for _, first, last in parts) == block:
            found[i] = parts
    return found


def key_bias(bounds, key_starts, row_start):
    rows = QUERY_BLOCK_ROWS
    bounds = jnp.transpose(jnp.broadcast_to(bounds, (rows, rows)))
    query_pos = row_start + lax.broadcasted_iota(jnp.int32, (rows, rows), 0)
    bias = []
    for start in key_starts:
        key_pos = start + lax.broadcasted_iota(jnp.int32, (rows, rows), 1)
        ok = key_pos >= bounds
        if start == row_start:
            ok = ok & (key_pos <= query_pos)
        bias.append(jnp.where(ok, 0.0, masked_value))
    return jnp.concatenate(bias, axis=1)


def attend_blocks(wanted, blocks, queries, owns, priors, bounds_ref, outs, finished=None):
    rows = QUERY_BLOCK_ROWS
    width = owns[wanted[0]][0][0].shape[1] // 2
    kv_heads, group = width // HEAD_SIZE, outs[wanted[0]][0].shape[1] // width
    keys = {
        b: [part for i in range(b, blocks) for part in priors[i]] + [part for i in range(b + 1) for part in owns[i]]
        for b in wanted
    }
    bias = {
        b: key_bias(
            bounds_ref[b : b + 1, :],
            [(i - blocks) * rows for i in range(b, blocks)] + [i * rows for i in range(b + 1)],
            b * rows,
        )
        for b in wanted
    }
    steps = [(b, n) for b in wanted for n in range(kv_heads)]
    lane = lax.broadcasted_iota(jnp.int32, (rows, HEAD_SIZE), 1)
    highests = {b: jnp.zeros((rows, HEAD_SIZE), jnp.float32) for b in wanted}
    totals = {b: jnp.ones((rows, HEAD_SIZE), jnp.float32) for b in wanted}

    def columns(parts, first):
        return jnp.concatenate([ref[i:j, first : first + HEAD_SIZE] for ref, i, j in parts], axis=0)

    def score(b, n):
        heads = range(n * group, (n + 1) * group)
        stacked = jnp.concatenate([columns(queries[b], h * HEAD_SIZE) for h in heads], axis=0)
        return lax.dot_general(
            stacked, columns(keys[b], n * HEAD_SIZE), (((1,), (1,)), ((), ())), preferred_element_type=jnp.float32
        )

    def weigh(b, scores):
        shape = scores.shape
        scores = (scores.reshape(group, rows, shape[1]) + bias[b][None]).reshape(shape)
        highest = jnp.max(scores, axis=1, keepdims=True)
        return highest, jnp.exp2(scores - highest)

    def finish(b, n, highest, weights):
        total = jnp.sum(weights, axis=1, keepdims=True)
        summed = jnp.dot(
            weights.astype(jnp.bfloat16),
            columns(keys[b], width + n * HEAD_SIZE),
            preferred_element_type=jnp.float32,
        )
        result = (summed / total).astype(jnp.bfloat16)
        for g in range(group):
            h, part = n * group + g, slice(g * rows, (g + 1) * rows)
            ref, at = outs[b]
            ref[at : at + rows, h * HEAD_SIZE : (h + 1) * HEAD_SIZE] = result[part]
            highests[b] = jnp.where(lane == h, highest[part], highests[b])
            totals[b] = jnp.where(lane == h, total[part], totals[b])
        if finished is not None and n == kv_heads - 1:
            finished(b)

    scores, pending = score(*steps[0]), None
    for i, (b, n) in enumerate(steps):
        ahead = score(*steps[i + 1]) if i + 1 < len(steps) else None
        highest, weights = weigh(b, scores)
        if pending is not None:
            finish(*pending)
        pending, scores = (b, n, highest, weights), ahead
    finish(*pending)
    return {
        b: jnp.transpose((highests[b] + jnp.log2(totals[b])) * math.log(2.0))[: kv_heads * group, :] for b in wanted
    }


def attention_kernel(chunks, wanted, *refs):
    count = len(chunks)
    prior_count = len(refs) - 2 * count - 3
    queries = block_parts(refs[:count], chunks)
    owns = block_parts(refs[count : 2 * count], chunks)
    priors = block_parts(refs[2 * count : -3], chunks[:prior_count])
    bounds_ref, out_ref, lse_ref = refs[-3:]
    outs = {b: (out_ref, (b - wanted[0]) * QUERY_BLOCK_ROWS) for b in wanted}
    lses = attend_blocks(wanted, chunks[0][1] // QUERY_BLOCK_ROWS, queries, owns, priors, bounds_ref, outs)
    for b in wanted:
        lse_ref[b - wanted[0]] = lses[b]


def last_attention_kernel(chunks, servers, server_ref, *refs):
    count, rows = len(chunks), QUERY_BLOCK_ROWS
    blocks = chunks[0][1] // rows
    queries = block_parts(refs[:count], chunks)
    owns = block_parts(refs[count : 2 * count], chunks)
    priors = block_parts(refs[2 * count : 3 * count], chunks)
    bounds_ref, *ready, out_hbm, send_ref, here, sems = refs[3 * count :]
    lses, copies = {}, []
    for i in range(0, len(ready), 2):
        out_ref, lse_ref = ready[i : i + 2]
        low = 1 + len(lses)
        lses.update({low + j: lse_ref[j] for j in range(lse_ref.shape[0])})
        place = out_hbm.at[pl.ds(low * rows, out_ref.shape[0]), :]
        copies.append(pltpu.make_async_copy(out_ref, place, sems.at[len(copies)]))
        copies[-1].start()

    def finished(block):
        copies.append(pltpu.make_async_copy(here, out_hbm.at[pl.ds(0, rows), :], sems.at[len(copies)]))
        copies[-1].start()

    lses.update(attend_blocks([0], blocks, queries, owns, priors, bounds_ref, {0: (here, 0)}, finished))
    for s in range(servers):
        value = jnp.full(lses[0].shape, jnp.inf, jnp.float32)
        for block, lse in lses.items():
            value = jnp.where(server_ref[block] == s, lse, value)
        send_ref[s] = value.astype(jnp.bfloat16)
    for copy in copies:
        copy.wait()


def pick_kernel(blocks, recv_ref, out_ref):
    shape = recv_ref.shape[1:]
    rank = jnp.zeros(shape, jnp.int32)
    picked = [jnp.zeros(shape, jnp.float32) for _ in range(blocks)]
    for i in range(recv_ref.shape[0]):
        value = recv_ref[i].astype(jnp.float32)
        valid = value < jnp.inf
        for k in range(blocks):
            picked[k] = jnp.where(valid & (rank == k), value, picked[k])
        rank = rank + valid.astype(jnp.int32)
    for k in range(blocks):
        out_ref[k] = picked[k]


def shards(tokens, norm_gain, w_query, w_key, value_matrix, doc_lengths, block_server):
    rows, features = tokens.shape
    width = w_key.shape[1]
    heads = w_query.shape[1] // HEAD_SIZE
    block = QUERY_BLOCK_ROWS
    blocks = rows // block
    servers = lax.axis_size("attn")
    sharers = lax.axis_size("proj")
    chips = sharers // CORES
    me_attn = lax.axis_index("attn")
    me_proj = lax.axis_index("proj")
    sibling = [(i, i ^ 1) for i in range(sharers)]

    def across(distance):
        return [(i, (i + distance * CORES) % sharers) for i in range(sharers)]

    middle = rows // 2
    chunks = [(middle, rows), (LAST_ROWS, middle), (0, LAST_ROWS)]
    arrived = []
    rest = tokens
    for low, high in chunks:
        piece = rest[low:high]
        if not arrived:
            piece, rest = lax.optimization_barrier((piece, rest))
        arrived.append([lax.ppermute(piece, "proj", across(d)) for d in range(1, chips)])
    other = lax.ppermute(tokens, "proj", sibling)

    order = [me_proj, me_proj ^ 1]
    for d in range(1, chips):
        source = (me_proj + sharers - d * CORES) % sharers
        order += [source, source ^ 1]
    order = jnp.stack([*order, me_attn * rows]).astype(jnp.int32)
    gains = norm_gain.reshape(sharers, features)

    w_key, value_matrix, w_query = [
        pltpu.with_memory_space_constraint(w, pltpu.HBM) for w in (w_key, value_matrix, w_query)
    ]
    q_acc, kv_acc, squares, bounds, wkv_rest, wq_rest = local_part(
        order, doc_lengths, tokens, other, gains, w_key, value_matrix, w_query
    )

    onward = [(i, (i + 1) % servers) for i in range(servers)]
    own, prior, queries = [], [], []
    tie = kv_acc
    for (low, high), sources in zip(chunks, arrived):
        sources, tie = lax.optimization_barrier((sources, tie))
        cuts = range(0, high - low, 64)
        groups = []
        for piece in sources:
            pieces = [piece[i:j] for i, j in zip(cuts, [*cuts[1:], piece.shape[0]])]
            groups += [[piece], [lax.ppermute(part, "proj", sibling) for part in pieces]]
        kv, q = project(high - low, low, order, groups, gains, wkv_rest, kv_acc, squares, wq_rest, q_acc)
        tie = q
        prior.append(lax.ppermute(kv, "attn", onward))
        own.append(kv)
        queries.append(q)

    queries = list(lax.optimization_barrier(tuple(queries)))

    def attend(wanted, priors):
        return pl.pallas_call(
            functools.partial(attention_kernel, chunks, wanted),
            out_shape=(
                jax.ShapeDtypeStruct((len(wanted) * block, heads * HEAD_SIZE), jnp.bfloat16),
                jax.ShapeDtypeStruct((len(wanted), heads, block), jnp.float32),
            ),
            in_specs=[VMEM] * (2 * len(chunks) + len(priors) + 1),
            out_specs=(VMEM, VMEM),
            compiler_params=params(24 << 20),
            cost_estimate=cost(),
        )(*queries, *own, *priors, bounds)

    above = attend(list(range(blocks // 2, blocks)), prior[:1])
    below = attend(list(range(1, blocks // 2)), prior[:2])
    out, send = pl.pallas_call(
        functools.partial(last_attention_kernel, chunks, servers),
        out_shape=(
            jax.ShapeDtypeStruct((rows, heads * HEAD_SIZE), jnp.bfloat16),
            jax.ShapeDtypeStruct((servers, heads, block), jnp.bfloat16),
        ),
        in_specs=[SMEM] + [VMEM] * (3 * len(chunks) + 5),
        out_specs=(HBM, VMEM),
        scratch_shapes=[pltpu.VMEM((block, heads * HEAD_SIZE), jnp.bfloat16), pltpu.SemaphoreType.DMA((3,))],
        compiler_params=params(24 << 20),
        cost_estimate=cost(),
    )(block_server, *queries, *own, *prior, bounds, *below, *above)
    recv = lax.all_to_all(send, "attn", split_axis=0, concat_axis=0, tiled=True)
    served = pl.pallas_call(
        functools.partial(pick_kernel, blocks),
        out_shape=jax.ShapeDtypeStruct((blocks, heads, block), jnp.float32),
        in_specs=[VMEM],
        out_specs=VMEM,
        compiler_params=params(),
    )(recv)
    return (out, served)


def solution(mesh):
    return jax.shard_map(
        shards,
        mesh=mesh,
        in_specs=(
            P("attn", "proj"),
            P(),
            P(None, "proj"),
            P(None, "proj"),
            P(None, "proj"),
            P(),
            P("attn"),
        ),
        out_specs=(P("attn", "proj"), P("attn", "proj", None)),
        check_vma=False,
    )
```

```python
import functools
import math

import jax
import jax.numpy as jnp
from jax import lax
from jax.experimental import pallas as pl
from jax.experimental.pallas import tpu as pltpu
from jax.sharding import PartitionSpec as P

HEAD_SIZE = 128
QUERY_BLOCK_ROWS = 128
CORES = 2

masked_value = -1e30
norm_eps = 1e-05
score_scale = 1.0 / HEAD_SIZE**0.5
log2_scale = score_scale * math.log2(math.e)

VMEM = pl.BlockSpec(memory_space=pltpu.VMEM)
SMEM = pl.BlockSpec(memory_space=pltpu.SMEM)
HBM = pl.BlockSpec(memory_space=pltpu.HBM)


def params(limit=16 << 20):
    return pltpu.CompilerParams(vmem_limit_bytes=limit)


def part_terms(x, gain):
    values = x.astype(jnp.float32)
    scaled = (values * gain).astype(jnp.bfloat16)
    return scaled, jnp.sum(values * values, axis=1, keepdims=True)


def cost():
    return pl.CostEstimate(flops=1 << 10, bytes_accessed=1 << 10, transcendentals=0)


def local_kernel(order_ref, docs_ref, server_ref, x_ref, other_ref, gain_ref, wk, wv, wq, *refs):
    q_ref, kv_ref, sq_ref, bound_ref, route_ref, gain_rest, kv_rest, q_rest, kv_own, q_own, sems = refs
    features, width = x_ref.shape[1], wk.shape[1]

    def fetch(slot, kv_to, q_to, place):
        rows = pl.ds(pl.multiple_of(order_ref[slot] * features, features), features)
        here = pl.ds(place * features, features)
        copies = (
            pltpu.make_async_copy(wk.at[rows, :], kv_to.at[here, pl.ds(0, width)], sems.at[slot, 0]),
            pltpu.make_async_copy(wv.at[rows, :], kv_to.at[here, pl.ds(width, width)], sems.at[slot, 1]),
            pltpu.make_async_copy(wq.at[rows, :], q_to.at[here, :], sems.at[slot, 2]),
        )
        for copy in copies:
            copy.start()
        return copies

    mine = [fetch(slot, kv_own, q_own, slot) for slot in range(CORES)]
    rest = [fetch(CORES + i, kv_rest, q_rest, i) for i in range(q_rest.shape[0] // features)]

    shape = bound_ref.shape
    base = order_ref[order_ref.shape[0] - 1]
    position = lax.broadcasted_iota(jnp.int32, shape, 0) * shape[1] + lax.broadcasted_iota(jnp.int32, shape, 1)
    start = -base
    bounds = jnp.full(shape, start, jnp.int32)
    for d in range(docs_ref.shape[0]):
        bounds = jnp.where(position >= start, start, bounds)
        start = start + docs_ref[d]
    bound_ref[...] = bounds
    for block in range(route_ref.shape[0]):
        route_ref[block] = jnp.full(route_ref.shape[1:], server_ref[block], jnp.int32)
    for i in range(gain_rest.shape[0]):
        gain_rest[i : i + 1, :] = gain_ref[pl.ds(order_ref[CORES + i], 1), :]

    parts = [
        part_terms(ref[...], gain_ref[pl.ds(order_ref[slot], 1), :]) for slot, ref in enumerate((x_ref, other_ref))
    ]
    sq_ref[...] = parts[0][1] + parts[1][1]
    scaled = jnp.concatenate([part[0] for part in parts], axis=1)
    for k, v, _ in mine:
        k.wait()
        v.wait()
    kv_ref[...] = jnp.dot(scaled, kv_own[...], preferred_element_type=jnp.float32)
    for _, _, q in mine:
        q.wait()
    q_ref[...] = jnp.dot(scaled, q_own[...], preferred_element_type=jnp.float32)
    for copies in rest:
        for copy in copies:
            copy.wait()


def local_part(order, docs, block_server, x, other, gains, wk, wv, wq):
    rows, features = x.shape
    q_width, kv_width = wq.shape[1], 2 * wk.shape[1]
    rest = wq.shape[0] - CORES * features
    return pl.pallas_call(
        local_kernel,
        out_shape=(
            pltpu.VMEM((rows, q_width), jnp.float32),
            pltpu.VMEM((rows, kv_width), jnp.float32),
            pltpu.VMEM((rows, 1), jnp.float32),
            pltpu.VMEM((rows // QUERY_BLOCK_ROWS, QUERY_BLOCK_ROWS), jnp.int32),
            pltpu.VMEM((rows // QUERY_BLOCK_ROWS, q_width // HEAD_SIZE, QUERY_BLOCK_ROWS), jnp.int32),
            pltpu.VMEM((rest // features, features), jnp.float32),
            pltpu.VMEM((rest, kv_width), jnp.bfloat16),
            pltpu.VMEM((rest, q_width), jnp.bfloat16),
        ),
        in_specs=[SMEM, SMEM, SMEM, VMEM, VMEM, VMEM, HBM, HBM, HBM],
        out_specs=(VMEM,) * 8,
        scratch_shapes=[
            pltpu.VMEM((CORES * features, kv_width), jnp.bfloat16),
            pltpu.VMEM((CORES * features, q_width), jnp.bfloat16),
            pltpu.SemaphoreType.DMA((wq.shape[0] // features, 3)),
        ],
        compiler_params=params(32 << 20),
        cost_estimate=cost(),
    )(order, docs, block_server, x, other, gains, wk, wv, wq)


def remote_rows(sizes, refs, gain_ref):
    terms = []
    for i, size in enumerate(sizes):
        x = jnp.concatenate([ref[...] for ref in refs[:size]], axis=0)
        refs = refs[size:]
        terms.append(part_terms(x, gain_ref[i : i + 1, :]))
    return jnp.concatenate([x for x, _ in terms], axis=1), sum(square for _, square in terms)


def chunk_kernel(sizes, row, kinds, *refs):
    pieces, (gain_ref, sq_ref, *refs) = refs[: sum(sizes)], refs[sum(sizes) :]
    scaled, squares = remote_rows(sizes, pieces, gain_ref)
    here = slice(row, row + scaled.shape[0])
    features = scaled.shape[1] // len(sizes)
    inverse = lax.rsqrt((sq_ref[here, :] + squares) / (features * (len(sizes) + CORES)) + norm_eps)
    for i, kind in enumerate(kinds):
        w_ref, acc_ref = refs[2 * i : 2 * i + 2]
        total = acc_ref[here, :] + jnp.dot(scaled, w_ref[...], preferred_element_type=jnp.float32)
        factor = inverse * log2_scale if kind == "q" else inverse
        refs[2 * len(kinds) + i][...] = (total * factor).astype(jnp.bfloat16)


def project(rows, row, groups, gains, squares, **sides):
    operands = [piece for group in groups for piece in group] + [gains, squares]
    for side in sides.values():
        operands += side
    return pl.pallas_call(
        functools.partial(chunk_kernel, [len(group) for group in groups], row, tuple(sides)),
        out_shape=tuple(jax.ShapeDtypeStruct((rows, w.shape[1]), jnp.bfloat16) for w, _ in sides.values()),
        in_specs=[VMEM] * len(operands),
        out_specs=(VMEM,) * len(sides),
        compiler_params=params(),
        cost_estimate=cost(),
    )(*operands)


def block_parts(refs, chunks):
    found = {}
    block = QUERY_BLOCK_ROWS
    for i in range(chunks[0][1] // block):
        parts = []
        for ref, (low, high) in zip(refs, chunks):
            first, last = max(low, i * block), min(high, (i + 1) * block)
            if first < last:
                parts.insert(0, (ref, first - low, last - low))
        if sum(last - first for _, first, last in parts) == block:
            found[i] = parts
    return found


def key_bias(bounds, key_starts, row_start):
    rows = QUERY_BLOCK_ROWS
    query_pos = row_start + lax.broadcasted_iota(jnp.int32, (rows, rows), 1)
    bias = []
    for start in key_starts:
        key_pos = start + lax.broadcasted_iota(jnp.int32, (rows, rows), 0)
        ok = key_pos >= bounds
        if start == row_start:
            ok = ok & (key_pos <= query_pos)
        bias.append(jnp.where(ok, 0.0, masked_value))
    return jnp.concatenate(bias, axis=0)


def attend_blocks(wanted, blocks, queries, owns, priors, bounds_ref, outs, lse_refs):
    rows = QUERY_BLOCK_ROWS
    width = owns[wanted[0]][0][0].shape[1] // 2
    kv_heads, group = width // HEAD_SIZE, outs[wanted[0]][0].shape[1] // width
    keys = {
        b: [part for i in range(b, blocks) for part in priors[i]] + [part for i in range(b + 1) for part in owns[i]]
        for b in wanted
    }
    bias = {}
    for b in wanted:
        starts = [(i - blocks) * rows for i in range(b, blocks)] + [i * rows for i in range(b + 1)]
        block_bias = key_bias(bounds_ref[b : b + 1, :], starts, b * rows)
        bias[b] = jnp.concatenate([block_bias] * group, axis=1)
    steps = [(b, n) for b in wanted for n in range(kv_heads)]

    def columns(parts, first):
        return jnp.concatenate([ref[i:j, first : first + HEAD_SIZE] for ref, i, j in parts], axis=0)

    def score(b, n):
        heads = range(n * group, (n + 1) * group)
        stacked = jnp.concatenate([columns(queries[b], h * HEAD_SIZE) for h in heads], axis=0)
        return lax.dot_general(
            columns(keys[b], n * HEAD_SIZE), stacked, (((1,), (1,)), ((), ())), preferred_element_type=jnp.float32
        )

    def weigh(b, scores):
        scores = scores + bias[b]
        highest = jnp.max(scores, axis=0, keepdims=True)
        return highest, jnp.exp2(scores - highest)

    def finish(b, n, highest, weights):
        total = jnp.sum(weights, axis=0, keepdims=True)
        summed = lax.dot_general(
            columns(keys[b], width + n * HEAD_SIZE),
            weights.astype(jnp.bfloat16),
            (((0,), (0,)), ((), ())),
            preferred_element_type=jnp.float32,
        )
        result = (summed / total).astype(jnp.bfloat16)
        lse = (highest + jnp.log2(total)) * math.log(2.0)
        ref, at = outs[b]
        for g in range(group):
            h, part = n * group + g, slice(g * rows, (g + 1) * rows)
            ref[at : at + rows, h * HEAD_SIZE : (h + 1) * HEAD_SIZE] = jnp.transpose(result[:, part])
            lse_refs[b][h : h + 1, :] = lse[:, part]

    scores, pending = score(*steps[0]), None
    for i, (b, n) in enumerate(steps):
        ahead = score(*steps[i + 1]) if i + 1 < len(steps) else None
        highest, weights = weigh(b, scores)
        if pending is not None:
            finish(*pending)
        pending, scores = (b, n, highest, weights), ahead
    finish(*pending)


def attention_refs(chunks, refs):
    count = len(chunks)
    queries = block_parts(refs[:count], chunks)
    owns = block_parts(refs[count : 2 * count], chunks)
    return queries, owns, refs[2 * count :]


def high_attention_kernel(chunks, wanted, *refs):
    queries, owns, (*priors, bounds_ref, out_ref, lse_ref) = attention_refs(chunks, refs)
    priors = block_parts(priors, chunks)
    outs = {b: (out_ref, (b - wanted[0]) * QUERY_BLOCK_ROWS) for b in wanted}
    lses = {b: lse_ref.at[b - wanted[0]] for b in wanted}
    attend_blocks(wanted, chunks[0][1] // QUERY_BLOCK_ROWS, queries, owns, priors, bounds_ref, outs, lses)


def low_attention_kernel(chunks, wanted, *refs):
    queries, owns, (*priors, bounds_ref, above_ref, out_ref, lse_ref, out_hbm, sem) = attention_refs(chunks, refs)
    priors = block_parts(priors, chunks)
    rows = pl.ds((wanted[-1] + 1) * QUERY_BLOCK_ROWS, above_ref.shape[0])
    copy = pltpu.make_async_copy(above_ref, out_hbm.at[rows, :], sem)
    copy.start()
    outs = {b: (out_ref, (b - wanted[0]) * QUERY_BLOCK_ROWS) for b in wanted}
    lses = {b: lse_ref.at[b - wanted[0]] for b in wanted}
    attend_blocks(wanted, chunks[0][1] // QUERY_BLOCK_ROWS, queries, owns, priors, bounds_ref, outs, lses)
    copy.wait()


def last_attention_kernel(chunks, servers, *refs):
    queries, owns, refs = attention_refs(chunks, refs)
    *priors, bounds_ref, route_ref, below_ref, below_lse, above_lse, _, out_hbm, here, send_ref, lse, sem = refs
    priors = block_parts(priors, chunks)
    rows = pl.ds(QUERY_BLOCK_ROWS, below_ref.shape[0])
    copy = pltpu.make_async_copy(below_ref, out_hbm.at[rows, :], sem)
    copy.start()
    attend_blocks([0], chunks[0][1] // QUERY_BLOCK_ROWS, queries, owns, priors, bounds_ref, {0: (here, 0)}, {0: lse})
    lses = [lse[...]] + [ref[i] for ref in (below_lse, above_lse) for i in range(ref.shape[0])]
    for s in range(servers):
        value = jnp.full(lses[0].shape, jnp.inf, jnp.float32)
        for block, rows in enumerate(lses):
            value = jnp.where(route_ref[block] == s, rows, value)
        send_ref[s] = value.astype(jnp.bfloat16)
    copy.wait()


def pick_kernel(blocks, recv_ref, here_ref, _, served_hbm, out_hbm, served, sems):
    here = pltpu.make_async_copy(here_ref, out_hbm.at[pl.ds(0, here_ref.shape[0]), :], sems.at[0])
    here.start()
    shape = recv_ref.shape[1:]
    rank = jnp.zeros(shape, jnp.int32)
    picked = [jnp.zeros(shape, jnp.float32) for _ in range(blocks)]
    for i in range(recv_ref.shape[0]):
        value = recv_ref[i].astype(jnp.float32)
        valid = value < jnp.inf
        for k in range(blocks):
            picked[k] = jnp.where(valid & (rank == k), value, picked[k])
        rank = rank + valid.astype(jnp.int32)
    for k in range(blocks):
        served[k] = picked[k]
    copy = pltpu.make_async_copy(served, served_hbm, sems.at[1])
    copy.start()
    copy.wait()
    here.wait()


def shards(tokens, norm_gain, w_query, w_key, value_matrix, doc_lengths, block_server):
    rows, features = tokens.shape
    width = w_key.shape[1]
    heads = w_query.shape[1] // HEAD_SIZE
    block = QUERY_BLOCK_ROWS
    blocks = rows // block
    servers = lax.axis_size("attn")
    sharers = lax.axis_size("proj")
    chips = sharers // CORES
    me_attn = lax.axis_index("attn")
    me_proj = lax.axis_index("proj")
    sibling = [(i, i ^ 1) for i in range(sharers)]

    def across(distance):
        return [(i, (i + distance * CORES) % sharers) for i in range(sharers)]

    middle = blocks // 2
    chunks = [(middle * block, rows)] + [(i * block, (i + 1) * block) for i in reversed(range(middle))]
    arrived = []
    rest = tokens
    for low, high in chunks:
        piece = rest[low:high]
        if not arrived:
            piece, rest = lax.optimization_barrier((piece, rest))
        arrived.append([lax.ppermute(piece, "proj", across(d)) for d in range(1, chips)])
    other = lax.ppermute(tokens, "proj", sibling)

    order = [me_proj, me_proj ^ 1]
    for d in range(1, chips):
        source = (me_proj + sharers - d * CORES) % sharers
        order += [source, source ^ 1]
    order = jnp.stack([*order, me_attn * rows]).astype(jnp.int32)
    gains = norm_gain.reshape(sharers, features)

    w_key, value_matrix, w_query = [
        pltpu.with_memory_space_constraint(w, pltpu.HBM) for w in (w_key, value_matrix, w_query)
    ]
    q_acc, kv_acc, squares, bounds, routes, gain_rest, wkv_rest, wq_rest = local_part(
        order, doc_lengths, block_server, tokens, other, gains, w_key, value_matrix, w_query
    )

    onward = [(i, (i + 1) % servers) for i in range(servers)]
    own, prior, queries = [], [], []
    tie = kv_acc
    for (low, high), sources in zip(chunks, arrived):
        sources, tie = lax.optimization_barrier((sources, tie))
        cuts = range(0, high - low, 64)
        groups = []
        for piece in sources:
            pieces = [piece[i:j] for i, j in zip(cuts, [*cuts[1:], piece.shape[0]])]
            groups += [[piece], [lax.ppermute(part, "proj", sibling) for part in pieces]]
        rest = (high - low, low, groups, gain_rest, squares)
        if low:
            kv, q = project(*rest, k=(wkv_rest, kv_acc), q=(wq_rest, q_acc))
        else:
            (kv,) = project(*rest, k=(wkv_rest, kv_acc))
            (q,) = project(*rest, q=(wq_rest, q_acc))
        tie = q
        prior.append(lax.ppermute(kv, "attn", onward))
        own.append(kv)
        queries.append(q)

    queries = list(lax.optimization_barrier(tuple(queries)))

    operands = (*queries, *own)
    width = heads * HEAD_SIZE

    def results(count):
        return (
            jax.ShapeDtypeStruct((count * block, width), jnp.bfloat16),
            jax.ShapeDtypeStruct((count, heads, block), jnp.float32),
        )

    whole = jax.ShapeDtypeStruct((rows, width), jnp.bfloat16)
    above, above_lse = pl.pallas_call(
        functools.partial(high_attention_kernel, chunks, list(range(middle, blocks))),
        out_shape=results(blocks - middle),
        in_specs=[VMEM] * (len(operands) + 2),
        out_specs=(VMEM, VMEM),
        compiler_params=params(24 << 20),
        cost_estimate=cost(),
    )(*operands, prior[0], bounds)
    below, below_lse, out = pl.pallas_call(
        functools.partial(low_attention_kernel, chunks, list(range(1, middle))),
        out_shape=(*results(middle - 1), whole),
        in_specs=[VMEM] * (len(operands) + len(prior) + 1),
        out_specs=(VMEM, VMEM, HBM),
        scratch_shapes=[pltpu.SemaphoreType.DMA],
        compiler_params=params(24 << 20),
        cost_estimate=cost(),
    )(*operands, *prior[:-1], bounds, above)
    out, here, send = pl.pallas_call(
        functools.partial(last_attention_kernel, chunks, servers),
        out_shape=(
            whole,
            results(1)[0],
            jax.ShapeDtypeStruct((servers, heads, block), jnp.bfloat16),
        ),
        in_specs=[VMEM] * (len(operands) + len(prior) + 5) + [HBM],
        out_specs=(HBM, VMEM, VMEM),
        scratch_shapes=[pltpu.VMEM((heads, block), jnp.float32), pltpu.SemaphoreType.DMA],
        input_output_aliases={len(operands) + len(prior) + 5: 0},
        compiler_params=params(24 << 20),
        cost_estimate=cost(),
    )(*operands, *prior, bounds, routes, below, below_lse, above_lse, out)
    recv = lax.all_to_all(send, "attn", split_axis=0, concat_axis=0, tiled=True)
    served, out = pl.pallas_call(
        functools.partial(pick_kernel, blocks),
        out_shape=(
            jax.ShapeDtypeStruct((blocks, heads, block), jnp.float32),
            jax.ShapeDtypeStruct((rows, heads * HEAD_SIZE), jnp.bfloat16),
        ),
        in_specs=[VMEM, VMEM, HBM],
        out_specs=(HBM, HBM),
        scratch_shapes=[pltpu.VMEM((blocks, heads, block), jnp.float32), pltpu.SemaphoreType.DMA((2,))],
        input_output_aliases={2: 1},
        compiler_params=params(),
    )(recv, here, out)
    return (out, served)


def solution(mesh):
    return jax.shard_map(
        shards,
        mesh=mesh,
        in_specs=(
            P("attn", "proj"),
            P(),
            P(None, "proj"),
            P(None, "proj"),
            P(None, "proj"),
            P(),
            P("attn"),
        ),
        out_specs=(P("attn", "proj"), P("attn", "proj", None)),
        check_vma=False,
    )
```

```python
import functools
import math

import jax
import jax.numpy as jnp
from jax import lax
from jax.experimental import pallas as pl
from jax.experimental.pallas import tpu as pltpu
from jax.sharding import PartitionSpec as P

HEAD_SIZE = 128
QUERY_BLOCK_ROWS = 128
CORES = 2

masked_value = -1e30
norm_eps = 1e-05
score_scale = 1.0 / HEAD_SIZE**0.5
log2_scale = score_scale * math.log2(math.e)

VMEM = pl.BlockSpec(memory_space=pltpu.VMEM)
SMEM = pl.BlockSpec(memory_space=pltpu.SMEM)
HBM = pl.BlockSpec(memory_space=pltpu.HBM)


def params(limit=16 << 20):
    return pltpu.CompilerParams(vmem_limit_bytes=limit)


def part_terms(x, gain):
    values = x.astype(jnp.float32)
    scaled = (values * gain).astype(jnp.bfloat16)
    return scaled, jnp.sum(values * values, axis=1, keepdims=True)


def cost():
    return pl.CostEstimate(flops=1 << 10, bytes_accessed=1 << 10, transcendentals=0)


def local_kernel(order_ref, docs_ref, server_ref, x_ref, other_ref, gain_ref, wk, wv, wq, *refs):
    q_ref, kv_ref, sq_ref, bound_ref, route_ref, gain_rest, kv_rest, q_rest, kv_own, q_own, sems = refs
    features, width = x_ref.shape[1], wk.shape[1]

    def fetch(slot, kv_to, q_to, place):
        rows = pl.ds(pl.multiple_of(order_ref[slot] * features, features), features)
        here = pl.ds(place * features, features)
        copies = (
            pltpu.make_async_copy(wk.at[rows, :], kv_to.at[here, pl.ds(0, width)], sems.at[slot, 0]),
            pltpu.make_async_copy(wv.at[rows, :], kv_to.at[here, pl.ds(width, width)], sems.at[slot, 1]),
            pltpu.make_async_copy(wq.at[rows, :], q_to.at[here, :], sems.at[slot, 2]),
        )
        for copy in copies:
            copy.start()
        return copies

    mine = [fetch(slot, kv_own, q_own, slot) for slot in range(CORES)]
    rest = [fetch(CORES + i, kv_rest, q_rest, i) for i in range(q_rest.shape[0] // features)]

    shape = bound_ref.shape
    base = order_ref[order_ref.shape[0] - 1]
    position = lax.broadcasted_iota(jnp.int32, shape, 0) * shape[1] + lax.broadcasted_iota(jnp.int32, shape, 1)
    start = -base
    bounds = jnp.full(shape, start, jnp.int32)
    for d in range(docs_ref.shape[0]):
        bounds = jnp.where(position >= start, start, bounds)
        start = start + docs_ref[d]
    bound_ref[...] = bounds
    for block in range(route_ref.shape[0]):
        route_ref[block] = jnp.full(route_ref.shape[1:], server_ref[block], jnp.int32)
    for i in range(gain_rest.shape[0]):
        gain_rest[i : i + 1, :] = gain_ref[pl.ds(order_ref[CORES + i], 1), :]

    parts = [
        part_terms(ref[...], gain_ref[pl.ds(order_ref[slot], 1), :]) for slot, ref in enumerate((x_ref, other_ref))
    ]
    sq_ref[...] = parts[0][1] + parts[1][1]
    scaled = jnp.concatenate([part[0] for part in parts], axis=1)
    for k, v, _ in mine:
        k.wait()
        v.wait()
    kv_ref[...] = jnp.dot(scaled, kv_own[...], preferred_element_type=jnp.float32)
    for _, _, q in mine:
        q.wait()
    q_ref[...] = jnp.dot(scaled, q_own[...], preferred_element_type=jnp.float32)
    for copies in rest:
        for copy in copies:
            copy.wait()


def local_part(order, docs, block_server, x, other, gains, wk, wv, wq):
    rows, features = x.shape
    q_width, kv_width = wq.shape[1], 2 * wk.shape[1]
    rest = wq.shape[0] - CORES * features
    return pl.pallas_call(
        local_kernel,
        out_shape=(
            pltpu.VMEM((rows, q_width), jnp.float32),
            pltpu.VMEM((rows, kv_width), jnp.float32),
            pltpu.VMEM((rows, 1), jnp.float32),
            pltpu.VMEM((rows // QUERY_BLOCK_ROWS, QUERY_BLOCK_ROWS), jnp.int32),
            pltpu.VMEM((rows // QUERY_BLOCK_ROWS, q_width // HEAD_SIZE, QUERY_BLOCK_ROWS), jnp.int32),
            pltpu.VMEM((rest // features, features), jnp.float32),
            pltpu.VMEM((rest, kv_width), jnp.bfloat16),
            pltpu.VMEM((rest, q_width), jnp.bfloat16),
        ),
        in_specs=[SMEM, SMEM, SMEM, VMEM, VMEM, VMEM, HBM, HBM, HBM],
        out_specs=(VMEM,) * 8,
        scratch_shapes=[
            pltpu.VMEM((CORES * features, kv_width), jnp.bfloat16),
            pltpu.VMEM((CORES * features, q_width), jnp.bfloat16),
            pltpu.SemaphoreType.DMA((wq.shape[0] // features, 3)),
        ],
        compiler_params=params(32 << 20),
        cost_estimate=cost(),
    )(order, docs, block_server, x, other, gains, wk, wv, wq)


def remote_rows(sizes, refs, gain_ref):
    terms = []
    for i, size in enumerate(sizes):
        x = jnp.concatenate([ref[...] for ref in refs[:size]], axis=0)
        refs = refs[size:]
        terms.append(part_terms(x, gain_ref[i : i + 1, :]))
    return jnp.concatenate([x for x, _ in terms], axis=1), sum(square for _, square in terms)


def chunk_kernel(sizes, row, kinds, *refs):
    pieces, (gain_ref, sq_ref, *refs) = refs[: sum(sizes)], refs[sum(sizes) :]
    scaled, squares = remote_rows(sizes, pieces, gain_ref)
    here = slice(row, row + scaled.shape[0])
    features = scaled.shape[1] // len(sizes)
    inverse = lax.rsqrt((sq_ref[here, :] + squares) / (features * (len(sizes) + CORES)) + norm_eps)
    for i, kind in enumerate(kinds):
        w_ref, acc_ref = refs[2 * i : 2 * i + 2]
        total = acc_ref[here, :] + jnp.dot(scaled, w_ref[...], preferred_element_type=jnp.float32)
        factor = inverse * log2_scale if kind == "q" else inverse
        refs[2 * len(kinds) + i][...] = (total * factor).astype(jnp.bfloat16)


def project(rows, row, groups, gains, squares, **sides):
    operands = [piece for group in groups for piece in group] + [gains, squares]
    for side in sides.values():
        operands += side
    return pl.pallas_call(
        functools.partial(chunk_kernel, [len(group) for group in groups], row, tuple(sides)),
        out_shape=tuple(jax.ShapeDtypeStruct((rows, w.shape[1]), jnp.bfloat16) for w, _ in sides.values()),
        in_specs=[VMEM] * len(operands),
        out_specs=(VMEM,) * len(sides),
        compiler_params=params(),
        cost_estimate=cost(),
    )(*operands)


def block_parts(refs, chunks):
    found = {}
    block = QUERY_BLOCK_ROWS
    for i in range(chunks[0][1] // block):
        parts = []
        for ref, (low, high) in zip(refs, chunks):
            first, last = max(low, i * block), min(high, (i + 1) * block)
            if first < last:
                parts.insert(0, (ref, first - low, last - low))
        if sum(last - first for _, first, last in parts) == block:
            found[i] = parts
    return found


def key_bias(bounds, key_starts, row_start):
    rows = QUERY_BLOCK_ROWS
    query_pos = row_start + lax.broadcasted_iota(jnp.int32, (rows, rows), 1)
    bias = []
    for start in key_starts:
        key_pos = start + lax.broadcasted_iota(jnp.int32, (rows, rows), 0)
        ok = key_pos >= bounds
        if start == row_start:
            ok = ok & (key_pos <= query_pos)
        bias.append(jnp.where(ok, 0.0, masked_value))
    return jnp.concatenate(bias, axis=0)


def attend_blocks(wanted, blocks, queries, owns, priors, bounds_ref, outs, lse_refs, states=()):
    rows = QUERY_BLOCK_ROWS
    width = owns[wanted[0]][0][0].shape[1] // 2
    kv_heads, group = width // HEAD_SIZE, outs[wanted[0]][0].shape[1] // width
    keys, bias = {}, {}
    for b in wanted:
        before = [i for i in range(b, blocks) if i in priors]
        keys[b] = [part for i in before for part in priors[i]] + [part for i in range(b + 1) for part in owns[i]]
        starts = [(i - blocks) * rows for i in before] + [i * rows for i in range(b + 1)]
        block_bias = key_bias(bounds_ref[b : b + 1, :], starts, b * rows)
        bias[b] = jnp.concatenate([block_bias] * group, axis=1)
    steps = [(b, n) for b in wanted for n in range(kv_heads)]

    def columns(parts, first):
        return jnp.concatenate([ref[i:j, first : first + HEAD_SIZE] for ref, i, j in parts], axis=0)

    def score(b, n):
        heads = range(n * group, (n + 1) * group)
        stacked = jnp.concatenate([columns(queries[b], h * HEAD_SIZE) for h in heads], axis=0)
        return lax.dot_general(
            columns(keys[b], n * HEAD_SIZE), stacked, (((1,), (1,)), ((), ())), preferred_element_type=jnp.float32
        )

    def weigh(b, scores):
        scores = scores + bias[b]
        highest = jnp.max(scores, axis=0, keepdims=True)
        return highest, jnp.exp2(scores - highest)

    def finish(b, n, highest, weights):
        total = jnp.sum(weights, axis=0, keepdims=True)
        summed = lax.dot_general(
            columns(keys[b], width + n * HEAD_SIZE),
            weights.astype(jnp.bfloat16),
            (((0,), (0,)), ((), ())),
            preferred_element_type=jnp.float32,
        )
        if b == 0:
            for ref, value in zip(states, (highest, total, summed)):
                ref[n] = value
            return
        result = (summed / total).astype(jnp.bfloat16)
        lse = (highest + jnp.log2(total)) * math.log(2.0)
        ref, at = outs[b]
        for g in range(group):
            h, part = n * group + g, slice(g * rows, (g + 1) * rows)
            ref[at : at + rows, h * HEAD_SIZE : (h + 1) * HEAD_SIZE] = jnp.transpose(result[:, part])
            lse_refs[b][h : h + 1, :] = lse[:, part]

    scores, pending = score(*steps[0]), None
    for i, (b, n) in enumerate(steps):
        ahead = score(*steps[i + 1]) if i + 1 < len(steps) else None
        highest, weights = weigh(b, scores)
        if pending is not None:
            finish(*pending)
        pending, scores = (b, n, highest, weights), ahead
    finish(*pending)


def attention_refs(chunks, refs):
    count = len(chunks)
    queries = block_parts(refs[:count], chunks)
    owns = block_parts(refs[count : 2 * count], chunks)
    return queries, owns, refs[2 * count :]


def high_attention_kernel(chunks, wanted, *refs):
    queries, owns, (*priors, bounds_ref, out_ref, lse_ref) = attention_refs(chunks, refs)
    priors = block_parts(priors, chunks)
    outs = {b: (out_ref, (b - wanted[0]) * QUERY_BLOCK_ROWS) for b in wanted}
    lses = {b: lse_ref.at[b - wanted[0]] for b in wanted}
    attend_blocks(wanted, chunks[0][1] // QUERY_BLOCK_ROWS, queries, owns, priors, bounds_ref, outs, lses)


def low_attention_kernel(chunks, wanted, *refs):
    queries, owns, refs = attention_refs(chunks, refs)
    *priors, bounds_ref, above_ref, out_ref, lse_ref, highest_ref, total_ref, summed_ref, out_hbm, sem = refs
    states = (highest_ref, total_ref, summed_ref)
    priors = block_parts(priors, chunks)
    rows = pl.ds((wanted[-1] + 1) * QUERY_BLOCK_ROWS, above_ref.shape[0])
    copy = pltpu.make_async_copy(above_ref, out_hbm.at[rows, :], sem)
    copy.start()
    outs = {b: (out_ref, (b - wanted[0]) * QUERY_BLOCK_ROWS) for b in wanted}
    lses = {b: lse_ref.at[b - wanted[0]] for b in wanted}
    blocks = chunks[0][1] // QUERY_BLOCK_ROWS
    attend_blocks([*wanted, 0], blocks, queries, owns, priors, bounds_ref, outs, lses, states)
    copy.wait()


def last_attention_kernel(blocks, servers, q_ref, prior_ref, bounds_ref, *refs):
    *states, route_ref, below_ref, below_lse, above_lse, _, out_hbm, here, send_ref, lse_ref, sem = refs
    block = QUERY_BLOCK_ROWS
    copy = pltpu.make_async_copy(below_ref, out_hbm.at[pl.ds(block, below_ref.shape[0]), :], sem)
    copy.start()
    width = prior_ref.shape[1] // 2
    group = q_ref.shape[1] // width
    bias = jnp.concatenate([key_bias(bounds_ref[:1, :], [-blocks * block], 0)] * group, axis=1)
    for n in range(width // HEAD_SIZE):
        heads = range(n * group, (n + 1) * group)
        stacked = jnp.concatenate([q_ref[:, h * HEAD_SIZE : (h + 1) * HEAD_SIZE] for h in heads], axis=0)
        scores = lax.dot_general(
            prior_ref[:, n * HEAD_SIZE : (n + 1) * HEAD_SIZE],
            stacked,
            (((1,), (1,)), ((), ())),
            preferred_element_type=jnp.float32,
        )
        scores = scores + bias
        highest, total, summed = (ref[n] for ref in states)
        top = jnp.maximum(highest, jnp.max(scores, axis=0, keepdims=True))
        weights = jnp.exp2(scores - top)
        scale = jnp.exp2(highest - top)
        total = total * scale + jnp.sum(weights, axis=0, keepdims=True)
        summed = summed * scale + lax.dot_general(
            prior_ref[:, width + n * HEAD_SIZE : width + (n + 1) * HEAD_SIZE],
            weights.astype(jnp.bfloat16),
            (((0,), (0,)), ((), ())),
            preferred_element_type=jnp.float32,
        )
        result = (summed / total).astype(jnp.bfloat16)
        lse = (top + jnp.log2(total)) * math.log(2.0)
        for g, h in enumerate(heads):
            part = slice(g * block, (g + 1) * block)
            here[:, h * HEAD_SIZE : (h + 1) * HEAD_SIZE] = jnp.transpose(result[:, part])
            lse_ref[h : h + 1, :] = lse[:, part]
    lses = [lse_ref[...]] + [ref[i] for ref in (below_lse, above_lse) for i in range(ref.shape[0])]
    for s in range(servers):
        value = jnp.full(lses[0].shape, jnp.inf, jnp.float32)
        for i, rows in enumerate(lses):
            value = jnp.where(route_ref[i] == s, rows, value)
        send_ref[s] = value.astype(jnp.bfloat16)
    copy.wait()


def pick_kernel(blocks, recv_ref, here_ref, _, served_hbm, out_hbm, served, sems):
    here = pltpu.make_async_copy(here_ref, out_hbm.at[pl.ds(0, here_ref.shape[0]), :], sems.at[0])
    here.start()
    shape = recv_ref.shape[1:]
    rank = jnp.zeros(shape, jnp.int32)
    picked = [jnp.zeros(shape, jnp.float32) for _ in range(blocks)]
    for i in range(recv_ref.shape[0]):
        value = recv_ref[i].astype(jnp.float32)
        valid = value < jnp.inf
        for k in range(blocks):
            picked[k] = jnp.where(valid & (rank == k), value, picked[k])
        rank = rank + valid.astype(jnp.int32)
    for k in range(blocks):
        served[k] = picked[k]
    copy = pltpu.make_async_copy(served, served_hbm, sems.at[1])
    copy.start()
    copy.wait()
    here.wait()


def shards(tokens, norm_gain, w_query, w_key, value_matrix, doc_lengths, block_server):
    rows, features = tokens.shape
    width = w_key.shape[1]
    heads = w_query.shape[1] // HEAD_SIZE
    block = QUERY_BLOCK_ROWS
    blocks = rows // block
    servers = lax.axis_size("attn")
    sharers = lax.axis_size("proj")
    chips = sharers // CORES
    me_attn = lax.axis_index("attn")
    me_proj = lax.axis_index("proj")
    sibling = [(i, i ^ 1) for i in range(sharers)]

    def across(distance):
        return [(i, (i + distance * CORES) % sharers) for i in range(sharers)]

    middle = blocks // 2
    chunks = [(middle * block, rows)] + [(i * block, (i + 1) * block) for i in reversed(range(middle))]
    arrived = []
    rest = tokens
    for low, high in chunks:
        piece = rest[low:high]
        if not arrived:
            piece, rest = lax.optimization_barrier((piece, rest))
        arrived.append([lax.ppermute(piece, "proj", across(d)) for d in range(1, chips)])
    other = lax.ppermute(tokens, "proj", sibling)

    order = [me_proj, me_proj ^ 1]
    for d in range(1, chips):
        source = (me_proj + sharers - d * CORES) % sharers
        order += [source, source ^ 1]
    order = jnp.stack([*order, me_attn * rows]).astype(jnp.int32)
    gains = norm_gain.reshape(sharers, features)

    w_key, value_matrix, w_query = [
        pltpu.with_memory_space_constraint(w, pltpu.HBM) for w in (w_key, value_matrix, w_query)
    ]
    q_acc, kv_acc, squares, bounds, routes, gain_rest, wkv_rest, wq_rest = local_part(
        order, doc_lengths, block_server, tokens, other, gains, w_key, value_matrix, w_query
    )

    onward = [(i, (i + 1) % servers) for i in range(servers)]
    own, prior, queries = [], [], []
    tie = kv_acc
    for (low, high), sources in zip(chunks, arrived):
        sources, tie = lax.optimization_barrier((sources, tie))
        cuts = range(0, high - low, 64)
        groups = []
        for piece in sources:
            pieces = [piece[i:j] for i, j in zip(cuts, [*cuts[1:], piece.shape[0]])]
            groups += [[piece], [lax.ppermute(part, "proj", sibling) for part in pieces]]
        rest = (high - low, low, groups, gain_rest, squares)
        if low:
            kv, q = project(*rest, k=(wkv_rest, kv_acc), q=(wq_rest, q_acc))
        else:
            (kv,) = project(*rest, k=(wkv_rest, kv_acc))
            (q,) = project(*rest, q=(wq_rest, q_acc))
        tie = q
        prior.append(lax.ppermute(kv, "attn", onward))
        own.append(kv)
        queries.append(q)

    queries = list(lax.optimization_barrier(tuple(queries)))

    operands = (*queries, *own)
    width = heads * HEAD_SIZE

    def results(count):
        return (
            jax.ShapeDtypeStruct((count * block, width), jnp.bfloat16),
            jax.ShapeDtypeStruct((count, heads, block), jnp.float32),
        )

    whole = jax.ShapeDtypeStruct((rows, width), jnp.bfloat16)
    above, above_lse = pl.pallas_call(
        functools.partial(high_attention_kernel, chunks, list(range(middle, blocks))),
        out_shape=results(blocks - middle),
        in_specs=[VMEM] * (len(operands) + 2),
        out_specs=(VMEM, VMEM),
        compiler_params=params(24 << 20),
        cost_estimate=cost(),
    )(*operands, prior[0], bounds)
    kv_heads = w_key.shape[1] // HEAD_SIZE
    lanes = heads // kv_heads * block
    states = tuple(jax.ShapeDtypeStruct((kv_heads, n, lanes), jnp.float32) for n in (1, 1, HEAD_SIZE))
    below, below_lse, *states, out = pl.pallas_call(
        functools.partial(low_attention_kernel, chunks, list(range(1, middle))),
        out_shape=(*results(middle - 1), *states, whole),
        in_specs=[VMEM] * (len(operands) + len(prior) + 1),
        out_specs=(VMEM,) * 5 + (HBM,),
        scratch_shapes=[pltpu.SemaphoreType.DMA],
        compiler_params=params(24 << 20),
        cost_estimate=cost(),
    )(*operands, *prior[:-1], bounds, above)
    out, here, send = pl.pallas_call(
        functools.partial(last_attention_kernel, blocks, servers),
        out_shape=(
            whole,
            results(1)[0],
            jax.ShapeDtypeStruct((servers, heads, block), jnp.bfloat16),
        ),
        in_specs=[VMEM] * 10 + [HBM],
        out_specs=(HBM, VMEM, VMEM),
        scratch_shapes=[pltpu.VMEM((heads, block), jnp.float32), pltpu.SemaphoreType.DMA],
        input_output_aliases={10: 0},
        compiler_params=params(24 << 20),
        cost_estimate=cost(),
    )(queries[-1], prior[-1], bounds, *states, routes, below, below_lse, above_lse, out)
    recv = lax.all_to_all(send, "attn", split_axis=0, concat_axis=0, tiled=True)
    served, out = pl.pallas_call(
        functools.partial(pick_kernel, blocks),
        out_shape=(
            jax.ShapeDtypeStruct((blocks, heads, block), jnp.float32),
            jax.ShapeDtypeStruct((rows, heads * HEAD_SIZE), jnp.bfloat16),
        ),
        in_specs=[VMEM, VMEM, HBM],
        out_specs=(HBM, HBM),
        scratch_shapes=[pltpu.VMEM((blocks, heads, block), jnp.float32), pltpu.SemaphoreType.DMA((2,))],
        input_output_aliases={2: 1},
        compiler_params=params(),
    )(recv, here, out)
    return (out, served)


def solution(mesh):
    return jax.shard_map(
        shards,
        mesh=mesh,
        in_specs=(
            P("attn", "proj"),
            P(),
            P(None, "proj"),
            P(None, "proj"),
            P(None, "proj"),
            P(),
            P("attn"),
        ),
        out_specs=(P("attn", "proj"), P("attn", "proj", None)),
        check_vma=False,
    )
```

```python
import functools
import math

import jax
import jax.numpy as jnp
from jax import lax
from jax.experimental import pallas as pl
from jax.experimental.pallas import tpu as pltpu
from jax.sharding import PartitionSpec as P

HEAD_SIZE = 128
QUERY_BLOCK_ROWS = 128
CORES = 2

masked_value = -1e30
norm_eps = 1e-05
score_scale = 1.0 / HEAD_SIZE**0.5
log2_scale = score_scale * math.log2(math.e)

VMEM = pl.BlockSpec(memory_space=pltpu.VMEM)
SMEM = pl.BlockSpec(memory_space=pltpu.SMEM)
HBM = pl.BlockSpec(memory_space=pltpu.HBM)


def params(limit=16 << 20):
    return pltpu.CompilerParams(vmem_limit_bytes=limit)


def part_terms(x, gain):
    values = x.astype(jnp.float32)
    scaled = (values * gain).astype(jnp.bfloat16)
    return scaled, jnp.sum(values * values, axis=1, keepdims=True)


def cost():
    return pl.CostEstimate(flops=1 << 10, bytes_accessed=1 << 10, transcendentals=0)


def local_kernel(order_ref, docs_ref, server_ref, x_ref, other_ref, gain_ref, wk, wv, wq, *refs):
    q_ref, kv_ref, sq_ref, bound_ref, route_ref, gain_rest, kv_rest, q_rest, kv_own, q_own, sems = refs
    features, width = x_ref.shape[1], wk.shape[1]

    def fetch(slot, kv_to, q_to, place):
        rows = pl.ds(pl.multiple_of(order_ref[slot] * features, features), features)
        here = pl.ds(place * features, features)
        copies = (
            pltpu.make_async_copy(wk.at[rows, :], kv_to.at[here, pl.ds(0, width)], sems.at[slot, 0]),
            pltpu.make_async_copy(wv.at[rows, :], kv_to.at[here, pl.ds(width, width)], sems.at[slot, 1]),
            pltpu.make_async_copy(wq.at[rows, :], q_to.at[here, :], sems.at[slot, 2]),
        )
        for copy in copies:
            copy.start()
        return copies

    mine = [fetch(slot, kv_own, q_own, slot) for slot in range(CORES)]
    rest = [fetch(CORES + i, kv_rest, q_rest, i) for i in range(q_rest.shape[0] // features)]

    shape = bound_ref.shape
    base = order_ref[order_ref.shape[0] - 1]
    position = lax.broadcasted_iota(jnp.int32, shape, 0) * shape[1] + lax.broadcasted_iota(jnp.int32, shape, 1)
    start = -base
    bounds = jnp.full(shape, start, jnp.int32)
    for d in range(docs_ref.shape[0]):
        bounds = jnp.where(position >= start, start, bounds)
        start = start + docs_ref[d]
    bound_ref[...] = bounds
    for block in range(route_ref.shape[0]):
        route_ref[block] = jnp.full(route_ref.shape[1:], server_ref[block], jnp.int32)
    for i in range(gain_rest.shape[0]):
        gain_rest[i : i + 1, :] = gain_ref[pl.ds(order_ref[CORES + i], 1), :]

    parts = [
        part_terms(ref[...], gain_ref[pl.ds(order_ref[slot], 1), :]) for slot, ref in enumerate((x_ref, other_ref))
    ]
    sq_ref[...] = parts[0][1] + parts[1][1]
    scaled = jnp.concatenate([part[0] for part in parts], axis=1)
    for k, v, _ in mine:
        k.wait()
        v.wait()
    kv_ref[...] = jnp.dot(scaled, kv_own[...], preferred_element_type=jnp.float32)
    for _, _, q in mine:
        q.wait()
    q_ref[...] = jnp.dot(scaled, q_own[...], preferred_element_type=jnp.float32)
    for copies in rest:
        for copy in copies:
            copy.wait()


def local_part(order, docs, block_server, x, other, gains, wk, wv, wq):
    rows, features = x.shape
    q_width, kv_width = wq.shape[1], 2 * wk.shape[1]
    rest = wq.shape[0] - CORES * features
    return pl.pallas_call(
        local_kernel,
        out_shape=(
            pltpu.VMEM((rows, q_width), jnp.float32),
            pltpu.VMEM((rows, kv_width), jnp.float32),
            pltpu.VMEM((rows, 1), jnp.float32),
            pltpu.VMEM((rows // QUERY_BLOCK_ROWS, QUERY_BLOCK_ROWS), jnp.int32),
            pltpu.VMEM((rows // QUERY_BLOCK_ROWS, q_width // HEAD_SIZE, QUERY_BLOCK_ROWS), jnp.int32),
            pltpu.VMEM((rest // features, features), jnp.float32),
            pltpu.VMEM((rest, kv_width), jnp.bfloat16),
            pltpu.VMEM((rest, q_width), jnp.bfloat16),
        ),
        in_specs=[SMEM, SMEM, SMEM, VMEM, VMEM, VMEM, HBM, HBM, HBM],
        out_specs=(VMEM,) * 8,
        scratch_shapes=[
            pltpu.VMEM((CORES * features, kv_width), jnp.bfloat16),
            pltpu.VMEM((CORES * features, q_width), jnp.bfloat16),
            pltpu.SemaphoreType.DMA((wq.shape[0] // features, 3)),
        ],
        compiler_params=params(32 << 20),
        cost_estimate=cost(),
    )(order, docs, block_server, x, other, gains, wk, wv, wq)


def remote_rows(sizes, refs, gain_ref):
    terms = []
    for i, size in enumerate(sizes):
        x = jnp.concatenate([ref[...] for ref in refs[:size]], axis=0)
        refs = refs[size:]
        terms.append(part_terms(x, gain_ref[i : i + 1, :]))
    return jnp.concatenate([x for x, _ in terms], axis=1), sum(square for _, square in terms)


def chunk_kernel(sizes, row, kinds, *refs):
    pieces, (gain_ref, sq_ref, *refs) = refs[: sum(sizes)], refs[sum(sizes) :]
    scaled, squares = remote_rows(sizes, pieces, gain_ref)
    here = slice(row, row + scaled.shape[0])
    features = scaled.shape[1] // len(sizes)
    inverse = lax.rsqrt((sq_ref[here, :] + squares) / (features * (len(sizes) + CORES)) + norm_eps)
    for i in range(kinds):
        w_ref, acc_ref = refs[2 * i : 2 * i + 2]
        total = acc_ref[here, :] + jnp.dot(scaled, w_ref[...], preferred_element_type=jnp.float32)
        refs[2 * kinds + i][...] = (total * inverse).astype(jnp.bfloat16)


def project(rows, row, groups, gains, squares, *sides):
    operands = [piece for group in groups for piece in group] + [gains, squares]
    for side in sides:
        operands += side
    return pl.pallas_call(
        functools.partial(chunk_kernel, [len(group) for group in groups], row, len(sides)),
        out_shape=tuple(jax.ShapeDtypeStruct((rows, w.shape[1]), jnp.bfloat16) for w, _ in sides),
        in_specs=[VMEM] * len(operands),
        out_specs=(VMEM,) * len(sides),
        compiler_params=params(),
        cost_estimate=cost(),
    )(*operands)


def block_parts(refs, chunks):
    found = {}
    block = QUERY_BLOCK_ROWS
    for i in range(chunks[0][1] // block):
        parts = []
        for ref, (low, high) in zip(refs, chunks):
            first, last = max(low, i * block), min(high, (i + 1) * block)
            if first < last:
                parts.insert(0, (ref, first - low, last - low))
        if sum(last - first for _, first, last in parts) == block:
            found[i] = parts
    return found


def score_caps(bounds, key_starts, row_start):
    rows = QUERY_BLOCK_ROWS
    query_pos = row_start + lax.broadcasted_iota(jnp.int32, (rows, rows), 1)
    caps = []
    for start in key_starts:
        key_pos = start + lax.broadcasted_iota(jnp.int32, (rows, rows), 0)
        ok = key_pos >= bounds
        if start == row_start:
            ok = ok & (key_pos <= query_pos)
        caps.append(jnp.where(ok, jnp.inf, masked_value))
    return jnp.concatenate(caps, axis=0)


def attend_blocks(wanted, blocks, queries, owns, priors, bounds_ref, outs, lse_refs, states=()):
    rows = QUERY_BLOCK_ROWS
    width = owns[wanted[0]][0][0].shape[1] // 2
    kv_heads, group = width // HEAD_SIZE, outs[wanted[0]][0].shape[1] // width
    keys, caps = {}, {}
    for b in wanted:
        before = [i for i in range(b, blocks) if i in priors]
        keys[b] = [part for i in before for part in priors[i]] + [part for i in range(b + 1) for part in owns[i]]
        starts = [(i - blocks) * rows for i in before] + [i * rows for i in range(b + 1)]
        caps[b] = jnp.concatenate([score_caps(bounds_ref[b : b + 1, :], starts, b * rows)] * group, axis=1)
    steps = [(b, n) for b in wanted for n in range(kv_heads)]

    def columns(parts, first):
        return jnp.concatenate([ref[i:j, first : first + HEAD_SIZE] for ref, i, j in parts], axis=0)

    def score(b, n):
        heads = range(n * group, (n + 1) * group)
        stacked = jnp.concatenate([columns(queries[b], h * HEAD_SIZE) for h in heads], axis=0)
        return lax.dot_general(
            columns(keys[b], n * HEAD_SIZE), stacked, (((1,), (1,)), ((), ())), preferred_element_type=jnp.float32
        )

    def weigh(b, scores):
        scores = jnp.minimum(scores, caps[b])
        highest = jnp.max(scores, axis=0, keepdims=True)
        return highest, jnp.exp2((scores - highest) * log2_scale)

    def finish(b, n, highest, weights):
        total = jnp.sum(weights, axis=0, keepdims=True)
        summed = lax.dot_general(
            columns(keys[b], width + n * HEAD_SIZE),
            weights.astype(jnp.bfloat16),
            (((0,), (0,)), ((), ())),
            preferred_element_type=jnp.float32,
        )
        if b == 0:
            for ref, value in zip(states, (highest, total, summed)):
                ref[n] = value
            return
        result = (summed / total).astype(jnp.bfloat16)
        lse = highest * score_scale + jnp.log(total)
        ref, at = outs[b]
        for g in range(group):
            h, part = n * group + g, slice(g * rows, (g + 1) * rows)
            ref[at : at + rows, h * HEAD_SIZE : (h + 1) * HEAD_SIZE] = jnp.transpose(result[:, part])
            lse_refs[b][h : h + 1, :] = lse[:, part]

    scores, pending = score(*steps[0]), None
    for i, (b, n) in enumerate(steps):
        ahead = score(*steps[i + 1]) if i + 1 < len(steps) else None
        highest, weights = weigh(b, scores)
        if pending is not None:
            finish(*pending)
        pending, scores = (b, n, highest, weights), ahead
    finish(*pending)


def attention_refs(chunks, refs):
    count = len(chunks)
    queries = block_parts(refs[:count], chunks)
    owns = block_parts(refs[count : 2 * count], chunks)
    return queries, owns, refs[2 * count :]


def merge_keys(n, prior_parts, query_parts, caps, states):
    width = prior_parts[0][0].shape[1] // 2
    group = query_parts[0][0].shape[1] // width

    def columns(parts, first):
        return jnp.concatenate([ref[i:j, first : first + HEAD_SIZE] for ref, i, j in parts], axis=0)

    heads = range(n * group, (n + 1) * group)
    stacked = jnp.concatenate([columns(query_parts, h * HEAD_SIZE) for h in heads], axis=0)
    scores = lax.dot_general(
        columns(prior_parts, n * HEAD_SIZE), stacked, (((1,), (1,)), ((), ())), preferred_element_type=jnp.float32
    )
    scores = jnp.minimum(scores, caps)
    highest, total, summed = (ref[n] for ref in states)
    top = jnp.maximum(highest, jnp.max(scores, axis=0, keepdims=True))
    weights = jnp.exp2((scores - top) * log2_scale)
    scale = jnp.exp2((highest - top) * log2_scale)
    total = total * scale + jnp.sum(weights, axis=0, keepdims=True)
    summed = summed * scale + lax.dot_general(
        columns(prior_parts, width + n * HEAD_SIZE),
        weights.astype(jnp.bfloat16),
        (((0,), (0,)), ((), ())),
        preferred_element_type=jnp.float32,
    )
    return top, total, summed


def prior_caps(bounds_ref, block, blocks, group):
    starts = [(block - blocks) * QUERY_BLOCK_ROWS]
    return jnp.concatenate([score_caps(bounds_ref[:1, :], starts, 0)] * group, axis=1)


def high_attention_kernel(chunks, wanted, *refs):
    queries, owns, refs = attention_refs(chunks, refs)
    prior_ref, bounds_ref, out_ref, lse_ref, *states = refs
    priors = block_parts([prior_ref], chunks)
    low, blocks = wanted[0], chunks[0][1] // QUERY_BLOCK_ROWS
    outs = {b: (out_ref, (b - low) * QUERY_BLOCK_ROWS) for b in wanted}
    lses = {b: lse_ref.at[b - low] for b in wanted}
    attend_blocks([*wanted, 0], blocks, queries, owns, priors, bounds_ref, outs, lses, states)


def low_attention_kernel(chunks, wanted, *refs):
    queries, owns, refs = attention_refs(chunks, refs)
    *refs, out_hbm, sem = refs
    *refs, out_ref, lse_ref, highest_ref, total_ref, summed_ref = refs
    *priors, bounds_ref, above_ref, highest, total, summed = refs
    priors = block_parts(priors, chunks)
    rows = pl.ds((wanted[-1] + 1) * QUERY_BLOCK_ROWS, above_ref.shape[0])
    copy = pltpu.make_async_copy(above_ref, out_hbm.at[rows, :], sem)
    copy.start()
    outs = {b: (out_ref, (b - wanted[0]) * QUERY_BLOCK_ROWS) for b in wanted}
    lses = {b: lse_ref.at[b - wanted[0]] for b in wanted}
    blocks = chunks[0][1] // QUERY_BLOCK_ROWS
    attend_blocks(wanted, blocks, queries, owns, priors, bounds_ref, outs, lses)
    kv_heads = highest.shape[0]
    group = highest.shape[2] // QUERY_BLOCK_ROWS
    for n in range(kv_heads):
        states = (highest, total, summed)
        for b in wanted:
            caps = prior_caps(bounds_ref, b, blocks, group)
            values = merge_keys(n, priors[b], queries[0], caps, states)
            states = (highest_ref, total_ref, summed_ref)
            for ref, value in zip(states, values):
                ref[n] = value
    copy.wait()


def last_attention_kernel(blocks, servers, q_ref, prior_ref, bounds_ref, *refs):
    *states, route_ref, below_ref, below_lse, above_lse, _, out_hbm, here, send_ref, lse_ref, sem = refs
    block = QUERY_BLOCK_ROWS
    copy = pltpu.make_async_copy(below_ref, out_hbm.at[pl.ds(block, below_ref.shape[0]), :], sem)
    copy.start()
    kv_heads = states[0].shape[0]
    group = states[0].shape[2] // block
    caps = prior_caps(bounds_ref, 0, blocks, group)
    for n in range(kv_heads):
        highest, total, summed = merge_keys(n, [(prior_ref, 0, block)], [(q_ref, 0, block)], caps, states)
        result = (summed / total).astype(jnp.bfloat16)
        lse = highest * score_scale + jnp.log(total)
        for g in range(group):
            h, part = n * group + g, slice(g * block, (g + 1) * block)
            here[:, h * HEAD_SIZE : (h + 1) * HEAD_SIZE] = jnp.transpose(result[:, part])
            lse_ref[h : h + 1, :] = lse[:, part]
    lses = [lse_ref[...]] + [ref[i] for ref in (below_lse, above_lse) for i in range(ref.shape[0])]
    for s in range(servers):
        value = jnp.full(lses[0].shape, jnp.inf, jnp.float32)
        for i, rows in enumerate(lses):
            value = jnp.where(route_ref[i] == s, rows, value)
        send_ref[s] = value.astype(jnp.bfloat16)
    copy.wait()


def pick_kernel(blocks, recv_ref, here_ref, _, served_hbm, out_hbm, served, sems):
    here = pltpu.make_async_copy(here_ref, out_hbm.at[pl.ds(0, here_ref.shape[0]), :], sems.at[0])
    here.start()
    shape = recv_ref.shape[1:]
    rank = jnp.zeros(shape, jnp.int32)
    picked = [jnp.zeros(shape, jnp.float32) for _ in range(blocks)]
    for i in range(recv_ref.shape[0]):
        value = recv_ref[i].astype(jnp.float32)
        valid = value < jnp.inf
        for k in range(blocks):
            picked[k] = jnp.where(valid & (rank == k), value, picked[k])
        rank = rank + valid.astype(jnp.int32)
    for k in range(blocks):
        served[k] = picked[k]
    copy = pltpu.make_async_copy(served, served_hbm, sems.at[1])
    copy.start()
    copy.wait()
    here.wait()


def shards(tokens, norm_gain, w_query, w_key, value_matrix, doc_lengths, block_server):
    rows, features = tokens.shape
    width = w_key.shape[1]
    heads = w_query.shape[1] // HEAD_SIZE
    block = QUERY_BLOCK_ROWS
    blocks = rows // block
    servers = lax.axis_size("attn")
    sharers = lax.axis_size("proj")
    chips = sharers // CORES
    me_attn = lax.axis_index("attn")
    me_proj = lax.axis_index("proj")
    sibling = [(i, i ^ 1) for i in range(sharers)]

    def across(distance):
        return [(i, (i + distance * CORES) % sharers) for i in range(sharers)]

    middle = blocks // 2
    chunks = [(middle * block, rows)] + [(i * block, (i + 1) * block) for i in reversed(range(middle))]
    arrived = []
    rest = tokens
    for low, high in chunks:
        piece = rest[low:high]
        if not arrived:
            piece, rest = lax.optimization_barrier((piece, rest))
        arrived.append([lax.ppermute(piece, "proj", across(d)) for d in range(1, chips)])
    other = lax.ppermute(tokens, "proj", sibling)

    order = [me_proj, me_proj ^ 1]
    for d in range(1, chips):
        source = (me_proj + sharers - d * CORES) % sharers
        order += [source, source ^ 1]
    order = jnp.stack([*order, me_attn * rows]).astype(jnp.int32)
    gains = norm_gain.reshape(sharers, features)

    w_key, value_matrix, w_query = [
        pltpu.with_memory_space_constraint(w, pltpu.HBM) for w in (w_key, value_matrix, w_query)
    ]
    q_acc, kv_acc, squares, bounds, routes, gain_rest, wkv_rest, wq_rest = local_part(
        order, doc_lengths, block_server, tokens, other, gains, w_key, value_matrix, w_query
    )

    onward = [(i, (i + 1) % servers) for i in range(servers)]
    own, prior, queries = [], [], []
    tie = kv_acc
    for (low, high), sources in zip(chunks, arrived):
        sources, tie = lax.optimization_barrier((sources, tie))
        cuts = range(0, high - low, 64)
        groups = []
        for piece in sources:
            pieces = [piece[i:j] for i, j in zip(cuts, [*cuts[1:], piece.shape[0]])]
            groups += [[piece], [lax.ppermute(part, "proj", sibling) for part in pieces]]
        rest = (high - low, low, groups, gain_rest, squares)
        if low:
            kv, q = project(*rest, (wkv_rest, kv_acc), (wq_rest, q_acc))
        else:
            (kv,) = project(*rest, (wkv_rest, kv_acc))
            (q,) = project(*rest, (wq_rest, q_acc))
        tie = q
        prior.append(lax.ppermute(kv, "attn", onward))
        own.append(kv)
        queries.append(q)

    queries = list(lax.optimization_barrier(tuple(queries)))

    operands = (*queries, *own)
    width = heads * HEAD_SIZE

    def results(count):
        return (
            jax.ShapeDtypeStruct((count * block, width), jnp.bfloat16),
            jax.ShapeDtypeStruct((count, heads, block), jnp.float32),
        )

    whole = jax.ShapeDtypeStruct((rows, width), jnp.bfloat16)
    kv_heads = w_key.shape[1] // HEAD_SIZE
    lanes = heads // kv_heads * block
    state_shapes = tuple(jax.ShapeDtypeStruct((kv_heads, n, lanes), jnp.float32) for n in (1, 1, HEAD_SIZE))
    above, above_lse, *states = pl.pallas_call(
        functools.partial(high_attention_kernel, chunks, list(range(middle, blocks))),
        out_shape=(*results(blocks - middle), *state_shapes),
        in_specs=[VMEM] * (len(operands) + 2),
        out_specs=(VMEM,) * 5,
        compiler_params=params(24 << 20),
        cost_estimate=cost(),
    )(*operands, prior[0], bounds)
    below, below_lse, *states, out = pl.pallas_call(
        functools.partial(low_attention_kernel, chunks, list(range(1, middle))),
        out_shape=(*results(middle - 1), *state_shapes, whole),
        in_specs=[VMEM] * (len(operands) + len(prior) + 4),
        out_specs=(VMEM,) * 5 + (HBM,),
        scratch_shapes=[pltpu.SemaphoreType.DMA],
        compiler_params=params(24 << 20),
        cost_estimate=cost(),
    )(*operands, *prior[:-1], bounds, above, *states)
    out, here, send = pl.pallas_call(
        functools.partial(last_attention_kernel, blocks, servers),
        out_shape=(
            whole,
            results(1)[0],
            jax.ShapeDtypeStruct((servers, heads, block), jnp.bfloat16),
        ),
        in_specs=[VMEM] * 10 + [HBM],
        out_specs=(HBM, VMEM, VMEM),
        scratch_shapes=[pltpu.VMEM((heads, block), jnp.float32), pltpu.SemaphoreType.DMA],
        input_output_aliases={10: 0},
        compiler_params=params(24 << 20),
        cost_estimate=cost(),
    )(queries[-1], prior[-1], bounds, *states, routes, below, below_lse, above_lse, out)
    recv = lax.all_to_all(send, "attn", split_axis=0, concat_axis=0, tiled=True)
    served, out = pl.pallas_call(
        functools.partial(pick_kernel, blocks),
        out_shape=(
            jax.ShapeDtypeStruct((blocks, heads, block), jnp.float32),
            jax.ShapeDtypeStruct((rows, heads * HEAD_SIZE), jnp.bfloat16),
        ),
        in_specs=[VMEM, VMEM, HBM],
        out_specs=(HBM, HBM),
        scratch_shapes=[pltpu.VMEM((blocks, heads, block), jnp.float32), pltpu.SemaphoreType.DMA((2,))],
        input_output_aliases={2: 1},
        compiler_params=params(),
    )(recv, here, out)
    return (out, served)


def solution(mesh):
    return jax.shard_map(
        shards,
        mesh=mesh,
        in_specs=(
            P("attn", "proj"),
            P(),
            P(None, "proj"),
            P(None, "proj"),
            P(None, "proj"),
            P(),
            P("attn"),
        ),
        out_specs=(P("attn", "proj"), P("attn", "proj", None)),
        check_vma=False,
    )
```

```python
import functools
import math

import jax
import jax.numpy as jnp
from jax import lax
from jax.experimental import pallas as pl
from jax.experimental.pallas import tpu as pltpu
from jax.sharding import PartitionSpec as P

HEAD_SIZE = 128
QUERY_BLOCK_ROWS = 128
CORES = 2

masked_value = -1e30
norm_eps = 1e-05
score_scale = 1.0 / HEAD_SIZE**0.5
log2_scale = score_scale * math.log2(math.e)

VMEM = pl.BlockSpec(memory_space=pltpu.VMEM)
SMEM = pl.BlockSpec(memory_space=pltpu.SMEM)
HBM = pl.BlockSpec(memory_space=pltpu.HBM)


def params(limit=16 << 20):
    return pltpu.CompilerParams(vmem_limit_bytes=limit)


def part_terms(x, gain):
    values = x.astype(jnp.float32)
    scaled = (values * gain).astype(jnp.bfloat16)
    return scaled, jnp.sum(values * values, axis=1, keepdims=True)


def cost():
    return pl.CostEstimate(flops=1 << 10, bytes_accessed=1 << 10, transcendentals=0)


def local_kernel(order_ref, docs_ref, server_ref, x_ref, other_ref, gain_ref, wk, wv, wq, *refs):
    q_ref, kv_ref, sq_ref, bound_ref, route_ref, gain_rest, kv_rest, q_rest, kv_own, q_own, sems = refs
    features, width = x_ref.shape[1], wk.shape[1]

    def fetch(slot, kv_to, q_to, place):
        rows = pl.ds(pl.multiple_of(order_ref[slot] * features, features), features)
        here = pl.ds(place * features, features)
        copies = (
            pltpu.make_async_copy(wk.at[rows, :], kv_to.at[here, pl.ds(0, width)], sems.at[slot, 0]),
            pltpu.make_async_copy(wv.at[rows, :], kv_to.at[here, pl.ds(width, width)], sems.at[slot, 1]),
            pltpu.make_async_copy(wq.at[rows, :], q_to.at[here, :], sems.at[slot, 2]),
        )
        for copy in copies:
            copy.start()
        return copies

    mine = [fetch(slot, kv_own, q_own, slot) for slot in range(CORES)]
    rest = [fetch(CORES + i, kv_rest, q_rest, i) for i in range(q_rest.shape[0] // features)]

    shape = bound_ref.shape
    base = order_ref[order_ref.shape[0] - 1]
    position = lax.broadcasted_iota(jnp.int32, shape, 0) * shape[1] + lax.broadcasted_iota(jnp.int32, shape, 1)
    start = -base
    bounds = jnp.full(shape, start, jnp.int32)
    for d in range(docs_ref.shape[0]):
        bounds = jnp.where(position >= start, start, bounds)
        start = start + docs_ref[d]
    bound_ref[...] = bounds
    for block in range(route_ref.shape[0]):
        route_ref[block] = jnp.full(route_ref.shape[1:], server_ref[block], jnp.int32)
    for i in range(gain_rest.shape[0]):
        gain_rest[i : i + 1, :] = gain_ref[pl.ds(order_ref[CORES + i], 1), :]

    parts = [
        part_terms(ref[...], gain_ref[pl.ds(order_ref[slot], 1), :]) for slot, ref in enumerate((x_ref, other_ref))
    ]
    sq_ref[...] = parts[0][1] + parts[1][1]
    scaled = jnp.concatenate([part[0] for part in parts], axis=1)
    for k, v, _ in mine:
        k.wait()
        v.wait()
    kv_ref[...] = jnp.dot(scaled, kv_own[...], preferred_element_type=jnp.float32)
    for _, _, q in mine:
        q.wait()
    q_ref[...] = jnp.dot(scaled, q_own[...], preferred_element_type=jnp.float32)
    for copies in rest:
        for copy in copies:
            copy.wait()


def local_part(order, docs, block_server, x, other, gains, wk, wv, wq):
    rows, features = x.shape
    q_width, kv_width = wq.shape[1], 2 * wk.shape[1]
    rest = wq.shape[0] - CORES * features
    return pl.pallas_call(
        local_kernel,
        out_shape=(
            pltpu.VMEM((rows, q_width), jnp.float32),
            pltpu.VMEM((rows, kv_width), jnp.float32),
            pltpu.VMEM((rows, 1), jnp.float32),
            pltpu.VMEM((rows // QUERY_BLOCK_ROWS, QUERY_BLOCK_ROWS), jnp.int32),
            pltpu.VMEM((rows // QUERY_BLOCK_ROWS, q_width // HEAD_SIZE, QUERY_BLOCK_ROWS), jnp.int32),
            pltpu.VMEM((rest // features, features), jnp.float32),
            pltpu.VMEM((rest, kv_width), jnp.bfloat16),
            pltpu.VMEM((rest, q_width), jnp.bfloat16),
        ),
        in_specs=[SMEM, SMEM, SMEM, VMEM, VMEM, VMEM, HBM, HBM, HBM],
        out_specs=(VMEM,) * 8,
        scratch_shapes=[
            pltpu.VMEM((CORES * features, kv_width), jnp.bfloat16),
            pltpu.VMEM((CORES * features, q_width), jnp.bfloat16),
            pltpu.SemaphoreType.DMA((wq.shape[0] // features, 3)),
        ],
        compiler_params=params(32 << 20),
        cost_estimate=cost(),
    )(order, docs, block_server, x, other, gains, wk, wv, wq)


def remote_rows(sizes, refs, gain_ref):
    terms = []
    for i, size in enumerate(sizes):
        x = jnp.concatenate([ref[...] for ref in refs[:size]], axis=0)
        refs = refs[size:]
        terms.append(part_terms(x, gain_ref[i : i + 1, :]))
    return jnp.concatenate([x for x, _ in terms], axis=1), sum(square for _, square in terms)


def chunk_kernel(sizes, row, kinds, *refs):
    pieces, (gain_ref, sq_ref, *refs) = refs[: sum(sizes)], refs[sum(sizes) :]
    scaled, squares = remote_rows(sizes, pieces, gain_ref)
    here = slice(row, row + scaled.shape[0])
    features = scaled.shape[1] // len(sizes)
    inverse = lax.rsqrt((sq_ref[here, :] + squares) / (features * (len(sizes) + CORES)) + norm_eps)
    for i in range(kinds):
        w_ref, acc_ref = refs[2 * i : 2 * i + 2]
        total = acc_ref[here, :] + jnp.dot(scaled, w_ref[...], preferred_element_type=jnp.float32)
        refs[2 * kinds + i][...] = (total * inverse).astype(jnp.bfloat16)


def project(rows, row, groups, gains, squares, *sides):
    operands = [piece for group in groups for piece in group] + [gains, squares]
    for side in sides:
        operands += side
    return pl.pallas_call(
        functools.partial(chunk_kernel, [len(group) for group in groups], row, len(sides)),
        out_shape=tuple(jax.ShapeDtypeStruct((rows, w.shape[1]), jnp.bfloat16) for w, _ in sides),
        in_specs=[VMEM] * len(operands),
        out_specs=(VMEM,) * len(sides),
        compiler_params=params(),
        cost_estimate=cost(),
    )(*operands)


def block_parts(refs, chunks):
    found = {}
    block = QUERY_BLOCK_ROWS
    for i in range(chunks[0][1] // block):
        parts = []
        for ref, (low, high) in zip(refs, chunks):
            first, last = max(low, i * block), min(high, (i + 1) * block)
            if first < last:
                parts.insert(0, (ref, first - low, last - low))
        if sum(last - first for _, first, last in parts) == block:
            found[i] = parts
    return found


def score_caps(bounds, key_starts, row_start):
    rows = QUERY_BLOCK_ROWS
    query_pos = row_start + lax.broadcasted_iota(jnp.int32, (rows, rows), 1)
    caps = []
    for start in key_starts:
        key_pos = start + lax.broadcasted_iota(jnp.int32, (rows, rows), 0)
        ok = key_pos >= bounds
        if start == row_start:
            ok = ok & (key_pos <= query_pos)
        caps.append(jnp.where(ok, jnp.inf, masked_value))
    return jnp.concatenate(caps, axis=0)


def attend_blocks(wanted, blocks, queries, owns, priors, bounds_ref, outs, lse_refs, states=()):
    rows = QUERY_BLOCK_ROWS
    width = owns[wanted[0]][0][0].shape[1] // 2
    kv_heads, group = width // HEAD_SIZE, outs[wanted[0]][0].shape[1] // width
    keys, caps = {}, {}
    for b in wanted:
        before = [i for i in range(b, blocks) if i in priors]
        keys[b] = [part for i in before for part in priors[i]] + [part for i in range(b + 1) for part in owns[i]]
        starts = [(i - blocks) * rows for i in before] + [i * rows for i in range(b + 1)]
        caps[b] = jnp.concatenate([score_caps(bounds_ref[b : b + 1, :], starts, b * rows)] * group, axis=1)
    steps = [(b, n) for b in wanted for n in range(kv_heads)]

    def columns(parts, first):
        return jnp.concatenate([ref[i:j, first : first + HEAD_SIZE] for ref, i, j in parts], axis=0)

    def score(b, n):
        heads = range(n * group, (n + 1) * group)
        stacked = jnp.concatenate([columns(queries[b], h * HEAD_SIZE) for h in heads], axis=0)
        return lax.dot_general(
            columns(keys[b], n * HEAD_SIZE), stacked, (((1,), (1,)), ((), ())), preferred_element_type=jnp.float32
        )

    def weigh(b, scores):
        scores = jnp.minimum(scores, caps[b])
        highest = jnp.max(scores, axis=0, keepdims=True)
        return highest, jnp.exp2((scores - highest) * log2_scale)

    def finish(b, n, highest, weights):
        total = jnp.sum(weights, axis=0, keepdims=True)
        summed = lax.dot_general(
            columns(keys[b], width + n * HEAD_SIZE),
            weights.astype(jnp.bfloat16),
            (((0,), (0,)), ((), ())),
            preferred_element_type=jnp.float32,
        )
        if b == 0:
            for ref, value in zip(states, (highest, total, summed)):
                ref[n] = value
            return
        result = (summed / total).astype(jnp.bfloat16)
        lse = highest * score_scale + jnp.log(total)
        ref, at = outs[b]
        for g in range(group):
            h, part = n * group + g, slice(g * rows, (g + 1) * rows)
            ref[at : at + rows, h * HEAD_SIZE : (h + 1) * HEAD_SIZE] = jnp.transpose(result[:, part])
            lse_refs[b][h : h + 1, :] = lse[:, part]

    scores, pending = score(*steps[0]), None
    for i, (b, n) in enumerate(steps):
        ahead = score(*steps[i + 1]) if i + 1 < len(steps) else None
        highest, weights = weigh(b, scores)
        if pending is not None:
            finish(*pending)
        pending, scores = (b, n, highest, weights), ahead
    finish(*pending)


def attention_refs(chunks, refs):
    count = len(chunks)
    queries = block_parts(refs[:count], chunks)
    owns = block_parts(refs[count : 2 * count], chunks)
    return queries, owns, refs[2 * count :]


def merge_keys(n, prior_parts, query_parts, caps, states):
    width = prior_parts[0][0].shape[1] // 2
    group = query_parts[0][0].shape[1] // width

    def columns(parts, first):
        return jnp.concatenate([ref[i:j, first : first + HEAD_SIZE] for ref, i, j in parts], axis=0)

    heads = range(n * group, (n + 1) * group)
    stacked = jnp.concatenate([columns(query_parts, h * HEAD_SIZE) for h in heads], axis=0)
    scores = lax.dot_general(
        columns(prior_parts, n * HEAD_SIZE), stacked, (((1,), (1,)), ((), ())), preferred_element_type=jnp.float32
    )
    scores = jnp.minimum(scores, caps)
    highest, total, summed = (ref[n] for ref in states)
    top = jnp.maximum(highest, jnp.max(scores, axis=0, keepdims=True))
    weights = jnp.exp2((scores - top) * log2_scale)
    scale = jnp.exp2((highest - top) * log2_scale)
    total = total * scale + jnp.sum(weights, axis=0, keepdims=True)
    summed = summed * scale + lax.dot_general(
        columns(prior_parts, width + n * HEAD_SIZE),
        weights.astype(jnp.bfloat16),
        (((0,), (0,)), ((), ())),
        preferred_element_type=jnp.float32,
    )
    return top, total, summed


def prior_caps(bounds_ref, block, blocks, group):
    starts = [(block - blocks) * QUERY_BLOCK_ROWS]
    return jnp.concatenate([score_caps(bounds_ref[:1, :], starts, 0)] * group, axis=1)


def high_attention_kernel(chunks, wanted, *refs):
    queries, owns, refs = attention_refs(chunks, refs)
    prior_ref, bounds_ref, out_ref, lse_ref, *states = refs
    priors = block_parts([prior_ref], chunks)
    low, blocks = wanted[0], chunks[0][1] // QUERY_BLOCK_ROWS
    outs = {b: (out_ref, (b - low) * QUERY_BLOCK_ROWS) for b in wanted}
    lses = {b: lse_ref.at[b - low] for b in wanted}
    attend_blocks([*wanted, 0], blocks, queries, owns, priors, bounds_ref, outs, lses, states)


def low_attention_kernel(chunks, wanted, *refs):
    queries, owns, refs = attention_refs(chunks, refs)
    *refs, out_hbm, sem = refs
    *refs, out_ref, lse_ref, highest_ref, total_ref, summed_ref = refs
    *priors, bounds_ref, above_ref, highest, total, summed = refs
    priors = block_parts(priors, chunks)
    rows = pl.ds((wanted[-1] + 1) * QUERY_BLOCK_ROWS, above_ref.shape[0])
    copy = pltpu.make_async_copy(above_ref, out_hbm.at[rows, :], sem)
    copy.start()
    outs = {b: (out_ref, (b - wanted[0]) * QUERY_BLOCK_ROWS) for b in wanted}
    lses = {b: lse_ref.at[b - wanted[0]] for b in wanted}
    blocks = chunks[0][1] // QUERY_BLOCK_ROWS
    attend_blocks(wanted, blocks, queries, owns, priors, bounds_ref, outs, lses)
    kv_heads = highest.shape[0]
    group = highest.shape[2] // QUERY_BLOCK_ROWS
    for n in range(kv_heads):
        states = (highest, total, summed)
        for b in wanted:
            caps = prior_caps(bounds_ref, b, blocks, group)
            values = merge_keys(n, priors[b], queries[0], caps, states)
            states = (highest_ref, total_ref, summed_ref)
            for ref, value in zip(states, values):
                ref[n] = value
    copy.wait()


def last_attention_kernel(blocks, servers, q_ref, prior_ref, bounds_ref, *refs):
    *states, route_ref, below_lse, above_lse, here, send_ref, lse_ref = refs
    block = QUERY_BLOCK_ROWS
    kv_heads = states[0].shape[0]
    group = states[0].shape[2] // block
    caps = prior_caps(bounds_ref, 0, blocks, group)
    for n in range(kv_heads):
        highest, total, summed = merge_keys(n, [(prior_ref, 0, block)], [(q_ref, 0, block)], caps, states)
        result = (summed / total).astype(jnp.bfloat16)
        lse = highest * score_scale + jnp.log(total)
        for g in range(group):
            h, part = n * group + g, slice(g * block, (g + 1) * block)
            here[:, h * HEAD_SIZE : (h + 1) * HEAD_SIZE] = jnp.transpose(result[:, part])
            lse_ref[h : h + 1, :] = lse[:, part]
    lses = [lse_ref[...]] + [ref[i] for ref in (below_lse, above_lse) for i in range(ref.shape[0])]
    for s in range(servers):
        value = jnp.full(lses[0].shape, jnp.inf, jnp.float32)
        for i, rows in enumerate(lses):
            value = jnp.where(route_ref[i] == s, rows, value)
        send_ref[s] = value.astype(jnp.bfloat16)


def pick_kernel(blocks, recv_ref, here_ref, below_ref, _, served_hbm, out_hbm, served, sems):
    here = pltpu.make_async_copy(here_ref, out_hbm.at[pl.ds(0, here_ref.shape[0]), :], sems.at[0])
    here.start()
    rows = pl.ds(here_ref.shape[0], below_ref.shape[0])
    below = pltpu.make_async_copy(below_ref, out_hbm.at[rows, :], sems.at[2])
    below.start()
    shape = recv_ref.shape[1:]
    rank = jnp.zeros(shape, jnp.int32)
    picked = [jnp.zeros(shape, jnp.float32) for _ in range(blocks)]
    for i in range(recv_ref.shape[0]):
        value = recv_ref[i].astype(jnp.float32)
        valid = value < jnp.inf
        for k in range(blocks):
            picked[k] = jnp.where(valid & (rank == k), value, picked[k])
        rank = rank + valid.astype(jnp.int32)
    for k in range(blocks):
        served[k] = picked[k]
    copy = pltpu.make_async_copy(served, served_hbm, sems.at[1])
    copy.start()
    copy.wait()
    here.wait()
    below.wait()


def shards(tokens, norm_gain, w_query, w_key, value_matrix, doc_lengths, block_server):
    rows, features = tokens.shape
    width = w_key.shape[1]
    heads = w_query.shape[1] // HEAD_SIZE
    block = QUERY_BLOCK_ROWS
    blocks = rows // block
    servers = lax.axis_size("attn")
    sharers = lax.axis_size("proj")
    chips = sharers // CORES
    me_attn = lax.axis_index("attn")
    me_proj = lax.axis_index("proj")
    sibling = [(i, i ^ 1) for i in range(sharers)]

    def across(distance):
        return [(i, (i + distance * CORES) % sharers) for i in range(sharers)]

    middle = blocks // 2
    chunks = [(middle * block, rows)] + [(i * block, (i + 1) * block) for i in reversed(range(middle))]
    arrived = []
    rest = tokens
    for low, high in chunks:
        piece = rest[low:high]
        if not arrived:
            piece, rest = lax.optimization_barrier((piece, rest))
        arrived.append([lax.ppermute(piece, "proj", across(d)) for d in range(1, chips)])
    other = lax.ppermute(tokens, "proj", sibling)

    order = [me_proj, me_proj ^ 1]
    for d in range(1, chips):
        source = (me_proj + sharers - d * CORES) % sharers
        order += [source, source ^ 1]
    order = jnp.stack([*order, me_attn * rows]).astype(jnp.int32)
    gains = norm_gain.reshape(sharers, features)

    w_key, value_matrix, w_query = [
        pltpu.with_memory_space_constraint(w, pltpu.HBM) for w in (w_key, value_matrix, w_query)
    ]
    q_acc, kv_acc, squares, bounds, routes, gain_rest, wkv_rest, wq_rest = local_part(
        order, doc_lengths, block_server, tokens, other, gains, w_key, value_matrix, w_query
    )

    onward = [(i, (i + 1) % servers) for i in range(servers)]
    own, prior, queries = [], [], []
    tie = kv_acc
    for (low, high), sources in zip(chunks, arrived):
        sources, tie = lax.optimization_barrier((sources, tie))
        cuts = range(0, high - low, 64)
        groups = []
        for piece in sources:
            pieces = [piece[i:j] for i, j in zip(cuts, [*cuts[1:], piece.shape[0]])]
            groups += [[piece], [lax.ppermute(part, "proj", sibling) for part in pieces]]
        rest = (high - low, low, groups, gain_rest, squares)
        if low:
            kv, q = project(*rest, (wkv_rest, kv_acc), (wq_rest, q_acc))
        else:
            (kv,) = project(*rest, (wkv_rest, kv_acc))
            (q,) = project(*rest, (wq_rest, q_acc))
        tie = q
        prior.append(lax.ppermute(kv, "attn", onward))
        own.append(kv)
        queries.append(q)

    queries = list(lax.optimization_barrier(tuple(queries)))

    operands = (*queries, *own)
    width = heads * HEAD_SIZE

    def results(count):
        return (
            jax.ShapeDtypeStruct((count * block, width), jnp.bfloat16),
            jax.ShapeDtypeStruct((count, heads, block), jnp.float32),
        )

    whole = jax.ShapeDtypeStruct((rows, width), jnp.bfloat16)
    kv_heads = w_key.shape[1] // HEAD_SIZE
    lanes = heads // kv_heads * block
    state_shapes = tuple(jax.ShapeDtypeStruct((kv_heads, n, lanes), jnp.float32) for n in (1, 1, HEAD_SIZE))
    above, above_lse, *states = pl.pallas_call(
        functools.partial(high_attention_kernel, chunks, list(range(middle, blocks))),
        out_shape=(*results(blocks - middle), *state_shapes),
        in_specs=[VMEM] * (len(operands) + 2),
        out_specs=(VMEM,) * 5,
        compiler_params=params(24 << 20),
        cost_estimate=cost(),
    )(*operands, prior[0], bounds)
    below, below_lse, *states, out = pl.pallas_call(
        functools.partial(low_attention_kernel, chunks, list(range(1, middle))),
        out_shape=(*results(middle - 1), *state_shapes, whole),
        in_specs=[VMEM] * (len(operands) + len(prior) + 4),
        out_specs=(VMEM,) * 5 + (HBM,),
        scratch_shapes=[pltpu.SemaphoreType.DMA],
        compiler_params=params(24 << 20),
        cost_estimate=cost(),
    )(*operands, *prior[:-1], bounds, above, *states)
    here, send = pl.pallas_call(
        functools.partial(last_attention_kernel, blocks, servers),
        out_shape=(results(1)[0], jax.ShapeDtypeStruct((servers, heads, block), jnp.bfloat16)),
        in_specs=[VMEM] * 9,
        out_specs=(VMEM, VMEM),
        scratch_shapes=[pltpu.VMEM((heads, block), jnp.float32)],
        compiler_params=params(24 << 20),
        cost_estimate=cost(),
    )(queries[-1], prior[-1], bounds, *states, routes, below_lse, above_lse)
    recv = lax.all_to_all(send, "attn", split_axis=0, concat_axis=0, tiled=True)
    served, out = pl.pallas_call(
        functools.partial(pick_kernel, blocks),
        out_shape=(
            jax.ShapeDtypeStruct((blocks, heads, block), jnp.float32),
            jax.ShapeDtypeStruct((rows, heads * HEAD_SIZE), jnp.bfloat16),
        ),
        in_specs=[VMEM, VMEM, VMEM, HBM],
        out_specs=(HBM, HBM),
        scratch_shapes=[pltpu.VMEM((blocks, heads, block), jnp.float32), pltpu.SemaphoreType.DMA((3,))],
        input_output_aliases={3: 1},
        compiler_params=params(),
    )(recv, here, below, out)
    return (out, served)


def solution(mesh):
    return jax.shard_map(
        shards,
        mesh=mesh,
        in_specs=(
            P("attn", "proj"),
            P(),
            P(None, "proj"),
            P(None, "proj"),
            P(None, "proj"),
            P(),
            P("attn"),
        ),
        out_specs=(P("attn", "proj"), P("attn", "proj", None)),
        check_vma=False,
    )
```

```python
import functools
import math

import jax
import jax.numpy as jnp
from jax import lax
from jax.experimental import pallas as pl
from jax.experimental.pallas import tpu as pltpu
from jax.sharding import PartitionSpec as P

HEAD_SIZE = 128
QUERY_BLOCK_ROWS = 128
CORES = 2

masked_value = -1e30
norm_eps = 1e-05
score_scale = 1.0 / HEAD_SIZE**0.5
log2_scale = score_scale * math.log2(math.e)

VMEM = pl.BlockSpec(memory_space=pltpu.VMEM)
SMEM = pl.BlockSpec(memory_space=pltpu.SMEM)
HBM = pl.BlockSpec(memory_space=pltpu.HBM)


def params(limit=16 << 20):
    return pltpu.CompilerParams(vmem_limit_bytes=limit)


def part_terms(x, gain):
    values = x.astype(jnp.float32)
    scaled = (values * gain).astype(jnp.bfloat16)
    return scaled, jnp.sum(values * values, axis=1, keepdims=True)


def cost():
    return pl.CostEstimate(flops=1 << 10, bytes_accessed=1 << 10, transcendentals=0)


def local_kernel(order_ref, docs_ref, server_ref, x_ref, other_ref, gain_ref, wk, wv, wq, *refs):
    q_ref, kv_ref, sq_ref, bound_ref, route_ref, gain_rest, kv_rest, q_rest, kv_own, q_own, sems = refs
    features, width = x_ref.shape[1], wk.shape[1]

    def fetch(slot, kv_to, q_to, place):
        rows = pl.ds(pl.multiple_of(order_ref[slot] * features, features), features)
        here = pl.ds(place * features, features)
        copies = (
            pltpu.make_async_copy(wk.at[rows, :], kv_to.at[here, pl.ds(0, width)], sems.at[slot, 0]),
            pltpu.make_async_copy(wv.at[rows, :], kv_to.at[here, pl.ds(width, width)], sems.at[slot, 1]),
            pltpu.make_async_copy(wq.at[rows, :], q_to.at[here, :], sems.at[slot, 2]),
        )
        for copy in copies:
            copy.start()
        return copies

    mine = [fetch(slot, kv_own, q_own, slot) for slot in range(CORES)]
    rest = [fetch(CORES + i, kv_rest, q_rest, i) for i in range(q_rest.shape[0] // features)]

    shape = bound_ref.shape
    base = order_ref[order_ref.shape[0] - 1]
    position = lax.broadcasted_iota(jnp.int32, shape, 0) * shape[1] + lax.broadcasted_iota(jnp.int32, shape, 1)
    start = -base
    bounds = jnp.full(shape, start, jnp.int32)
    for d in range(docs_ref.shape[0]):
        bounds = jnp.where(position >= start, start, bounds)
        start = start + docs_ref[d]
    bound_ref[...] = bounds
    for block in range(route_ref.shape[0]):
        route_ref[block] = jnp.full(route_ref.shape[1:], server_ref[block], jnp.int32)
    for i in range(gain_rest.shape[0]):
        gain_rest[i : i + 1, :] = gain_ref[pl.ds(order_ref[CORES + i], 1), :]

    parts = [
        part_terms(ref[...], gain_ref[pl.ds(order_ref[slot], 1), :]) for slot, ref in enumerate((x_ref, other_ref))
    ]
    sq_ref[...] = parts[0][1] + parts[1][1]
    scaled = jnp.concatenate([part[0] for part in parts], axis=1)
    for k, v, _ in mine:
        k.wait()
        v.wait()
    kv_ref[...] = jnp.dot(scaled, kv_own[...], preferred_element_type=jnp.float32)
    for _, _, q in mine:
        q.wait()
    q_ref[...] = jnp.dot(scaled, q_own[...], preferred_element_type=jnp.float32)
    for copies in rest:
        for copy in copies:
            copy.wait()


def local_part(order, docs, block_server, x, other, gains, wk, wv, wq):
    rows, features = x.shape
    q_width, kv_width = wq.shape[1], 2 * wk.shape[1]
    rest = wq.shape[0] - CORES * features
    return pl.pallas_call(
        local_kernel,
        out_shape=(
            pltpu.VMEM((rows, q_width), jnp.float32),
            pltpu.VMEM((rows, kv_width), jnp.float32),
            pltpu.VMEM((rows, 1), jnp.float32),
            pltpu.VMEM((rows // QUERY_BLOCK_ROWS, QUERY_BLOCK_ROWS), jnp.int32),
            pltpu.VMEM((rows // QUERY_BLOCK_ROWS, q_width // HEAD_SIZE, QUERY_BLOCK_ROWS), jnp.int32),
            pltpu.VMEM((rest // features, features), jnp.float32),
            pltpu.VMEM((rest, kv_width), jnp.bfloat16),
            pltpu.VMEM((rest, q_width), jnp.bfloat16),
        ),
        in_specs=[SMEM, SMEM, SMEM, VMEM, VMEM, VMEM, HBM, HBM, HBM],
        out_specs=(VMEM,) * 8,
        scratch_shapes=[
            pltpu.VMEM((CORES * features, kv_width), jnp.bfloat16),
            pltpu.VMEM((CORES * features, q_width), jnp.bfloat16),
            pltpu.SemaphoreType.DMA((wq.shape[0] // features, 3)),
        ],
        compiler_params=params(32 << 20),
        cost_estimate=cost(),
    )(order, docs, block_server, x, other, gains, wk, wv, wq)


def remote_rows(sizes, refs, gain_ref):
    terms = []
    for i, size in enumerate(sizes):
        x = jnp.concatenate([ref[...] for ref in refs[:size]], axis=0)
        refs = refs[size:]
        terms.append(part_terms(x, gain_ref[i : i + 1, :]))
    return jnp.concatenate([x for x, _ in terms], axis=1), sum(square for _, square in terms)


def chunk_kernel(sizes, row, kinds, *refs):
    pieces, (gain_ref, sq_ref, *refs) = refs[: sum(sizes)], refs[sum(sizes) :]
    scaled, squares = remote_rows(sizes, pieces, gain_ref)
    here = slice(row, row + scaled.shape[0])
    features = scaled.shape[1] // len(sizes)
    inverse = lax.rsqrt((sq_ref[here, :] + squares) / (features * (len(sizes) + CORES)) + norm_eps)
    for i in range(kinds):
        w_ref, acc_ref = refs[2 * i : 2 * i + 2]
        total = acc_ref[here, :] + jnp.dot(scaled, w_ref[...], preferred_element_type=jnp.float32)
        refs[2 * kinds + i][...] = (total * inverse).astype(jnp.bfloat16)


def project(rows, row, groups, gains, squares, *sides):
    operands = [piece for group in groups for piece in group] + [gains, squares]
    for side in sides:
        operands += side
    return pl.pallas_call(
        functools.partial(chunk_kernel, [len(group) for group in groups], row, len(sides)),
        out_shape=tuple(jax.ShapeDtypeStruct((rows, w.shape[1]), jnp.bfloat16) for w, _ in sides),
        in_specs=[VMEM] * len(operands),
        out_specs=(VMEM,) * len(sides),
        compiler_params=params(),
        cost_estimate=cost(),
    )(*operands)


def block_parts(refs, chunks):
    found = {}
    block = QUERY_BLOCK_ROWS
    for i in range(chunks[0][1] // block):
        parts = []
        for ref, (low, high) in zip(refs, chunks):
            first, last = max(low, i * block), min(high, (i + 1) * block)
            if first < last:
                parts.insert(0, (ref, first - low, last - low))
        if sum(last - first for _, first, last in parts) == block:
            found[i] = parts
    return found


def score_caps(bounds, key_starts, row_start):
    rows = QUERY_BLOCK_ROWS
    query_pos = row_start + lax.broadcasted_iota(jnp.int32, (rows, rows), 1)
    caps = []
    for start in key_starts:
        key_pos = start + lax.broadcasted_iota(jnp.int32, (rows, rows), 0)
        ok = key_pos >= bounds
        if start == row_start:
            ok = ok & (key_pos <= query_pos)
        caps.append(jnp.where(ok, jnp.inf, masked_value))
    return jnp.concatenate(caps, axis=0)


def attend_blocks(wanted, blocks, queries, owns, priors, bounds_ref, outs, lse_refs, states=()):
    rows = QUERY_BLOCK_ROWS
    width = owns[wanted[0]][0][0].shape[1] // 2
    kv_heads, group = width // HEAD_SIZE, outs[wanted[0]][0].shape[1] // width
    keys, caps = {}, {}
    for b in wanted:
        before = [i for i in range(b, blocks) if i in priors]
        keys[b] = [part for i in before for part in priors[i]] + [part for i in range(b + 1) for part in owns[i]]
        starts = [(i - blocks) * rows for i in before] + [i * rows for i in range(b + 1)]
        caps[b] = jnp.concatenate([score_caps(bounds_ref[b : b + 1, :], starts, b * rows)] * group, axis=1)
    steps = [(b, n) for b in wanted for n in range(kv_heads)]

    def columns(parts, first):
        return jnp.concatenate([ref[i:j, first : first + HEAD_SIZE] for ref, i, j in parts], axis=0)

    def score(b, n):
        heads = range(n * group, (n + 1) * group)
        stacked = jnp.concatenate([columns(queries[b], h * HEAD_SIZE) for h in heads], axis=0)
        return lax.dot_general(
            columns(keys[b], n * HEAD_SIZE), stacked, (((1,), (1,)), ((), ())), preferred_element_type=jnp.float32
        )

    def weigh(b, scores):
        scores = jnp.minimum(scores, caps[b])
        highest = jnp.max(scores, axis=0, keepdims=True)
        return highest, jnp.exp2((scores - highest) * log2_scale)

    def finish(b, n, highest, weights):
        total = jnp.sum(weights, axis=0, keepdims=True)
        summed = lax.dot_general(
            columns(keys[b], width + n * HEAD_SIZE),
            weights.astype(jnp.bfloat16),
            (((0,), (0,)), ((), ())),
            preferred_element_type=jnp.float32,
        )
        if b == 0:
            for ref, value in zip(states, (highest, total, summed)):
                ref[n] = value
            return
        result = (summed / total).astype(jnp.bfloat16)
        lse = highest * score_scale + jnp.log(total)
        ref, at = outs[b]
        for g in range(group):
            h, part = n * group + g, slice(g * rows, (g + 1) * rows)
            ref[at : at + rows, h * HEAD_SIZE : (h + 1) * HEAD_SIZE] = jnp.transpose(result[:, part])
            lse_refs[b][h : h + 1, :] = lse[:, part]

    scores, pending = score(*steps[0]), None
    for i, (b, n) in enumerate(steps):
        ahead = score(*steps[i + 1]) if i + 1 < len(steps) else None
        highest, weights = weigh(b, scores)
        if pending is not None:
            finish(*pending)
        pending, scores = (b, n, highest, weights), ahead
    finish(*pending)


def attention_refs(chunks, refs):
    count = len(chunks)
    queries = block_parts(refs[:count], chunks)
    owns = block_parts(refs[count : 2 * count], chunks)
    return queries, owns, refs[2 * count :]


def merge_keys(n, prior_parts, query_parts, caps, states):
    width = prior_parts[0][0].shape[1] // 2
    group = query_parts[0][0].shape[1] // width

    def columns(parts, first):
        return jnp.concatenate([ref[i:j, first : first + HEAD_SIZE] for ref, i, j in parts], axis=0)

    heads = range(n * group, (n + 1) * group)
    stacked = jnp.concatenate([columns(query_parts, h * HEAD_SIZE) for h in heads], axis=0)
    scores = lax.dot_general(
        columns(prior_parts, n * HEAD_SIZE), stacked, (((1,), (1,)), ((), ())), preferred_element_type=jnp.float32
    )
    scores = jnp.minimum(scores, caps)
    highest, total, summed = (ref[n] for ref in states)
    top = jnp.maximum(highest, jnp.max(scores, axis=0, keepdims=True))
    weights = jnp.exp2((scores - top) * log2_scale)
    scale = jnp.exp2((highest - top) * log2_scale)
    total = total * scale + jnp.sum(weights, axis=0, keepdims=True)
    summed = summed * scale + lax.dot_general(
        columns(prior_parts, width + n * HEAD_SIZE),
        weights.astype(jnp.bfloat16),
        (((0,), (0,)), ((), ())),
        preferred_element_type=jnp.float32,
    )
    return top, total, summed


def prior_caps(bounds_ref, block, blocks, group):
    starts = [(block - blocks) * QUERY_BLOCK_ROWS]
    return jnp.concatenate([score_caps(bounds_ref[:1, :], starts, 0)] * group, axis=1)


def high_attention_kernel(chunks, wanted, *refs):
    queries, owns, refs = attention_refs(chunks, refs)
    prior_ref, bounds_ref, out_ref, lse_ref, *states = refs
    priors = block_parts([prior_ref], chunks)
    low, blocks = wanted[0], chunks[0][1] // QUERY_BLOCK_ROWS
    outs = {b: (out_ref, (b - low) * QUERY_BLOCK_ROWS) for b in wanted}
    lses = {b: lse_ref.at[b - low] for b in wanted}
    attend_blocks([*wanted, 0], blocks, queries, owns, priors, bounds_ref, outs, lses, states)


def low_attention_kernel(chunks, wanted, *refs):
    queries, owns, refs = attention_refs(chunks, refs)
    *refs, out_hbm, sem = refs
    *refs, out_ref, lse_ref, highest_ref, total_ref, summed_ref = refs
    *priors, bounds_ref, above_ref, highest, total, summed = refs
    priors = block_parts(priors, chunks)
    rows = pl.ds((wanted[-1] + 1) * QUERY_BLOCK_ROWS, above_ref.shape[0])
    copy = pltpu.make_async_copy(above_ref, out_hbm.at[rows, :], sem)
    copy.start()
    outs = {b: (out_ref, (b - wanted[0]) * QUERY_BLOCK_ROWS) for b in wanted}
    lses = {b: lse_ref.at[b - wanted[0]] for b in wanted}
    blocks = chunks[0][1] // QUERY_BLOCK_ROWS
    attend_blocks(wanted, blocks, queries, owns, priors, bounds_ref, outs, lses)
    kv_heads = highest.shape[0]
    group = highest.shape[2] // QUERY_BLOCK_ROWS
    for n in range(kv_heads):
        states = (highest, total, summed)
        for b in wanted:
            caps = prior_caps(bounds_ref, b, blocks, group)
            values = merge_keys(n, priors[b], queries[0], caps, states)
            states = (highest_ref, total_ref, summed_ref)
            for ref, value in zip(states, values):
                ref[n] = value
    copy.wait()


def last_attention_kernel(blocks, servers, q_ref, prior_ref, bounds_ref, *refs):
    *states, route_ref, below_lse, above_lse, here, send_ref, lse_ref = refs
    block = QUERY_BLOCK_ROWS
    kv_heads = states[0].shape[0]
    group = states[0].shape[2] // block
    caps = prior_caps(bounds_ref, 0, blocks, group)
    for n in range(kv_heads):
        highest, total, summed = merge_keys(n, [(prior_ref, 0, block)], [(q_ref, 0, block)], caps, states)
        result = (summed / total).astype(jnp.bfloat16)
        lse = highest * score_scale + jnp.log(total)
        for g in range(group):
            h, part = n * group + g, slice(g * block, (g + 1) * block)
            here[:, h * HEAD_SIZE : (h + 1) * HEAD_SIZE] = jnp.transpose(result[:, part])
            lse_ref[h : h + 1, :] = lse[:, part]
    lses = [lse_ref[...]] + [ref[i] for ref in (below_lse, above_lse) for i in range(ref.shape[0])]
    for s in range(servers):
        value = jnp.full(lses[0].shape, jnp.inf, jnp.float32)
        for i, rows in enumerate(lses):
            value = jnp.where(route_ref[i] == s, rows, value)
        send_ref[s] = value.astype(jnp.bfloat16)


def pick_kernel(blocks, recv_ref, here_ref, below_ref, _, served_hbm, out_hbm, served, sems):
    here = pltpu.make_async_copy(here_ref, out_hbm.at[pl.ds(0, here_ref.shape[0]), :], sems.at[0])
    here.start()
    rows = pl.ds(here_ref.shape[0], below_ref.shape[0])
    below = pltpu.make_async_copy(below_ref, out_hbm.at[rows, :], sems.at[2])
    below.start()
    shape = recv_ref.shape[1:]
    rank = jnp.zeros(shape, jnp.int32)
    picked = [jnp.zeros(shape, jnp.float32) for _ in range(blocks)]
    for i in range(recv_ref.shape[0]):
        value = recv_ref[i].astype(jnp.float32)
        valid = value < jnp.inf
        for k in range(blocks):
            picked[k] = jnp.where(valid & (rank == k), value, picked[k])
        rank = rank + valid.astype(jnp.int32)
    for k in range(blocks):
        served[k] = picked[k]
    copy = pltpu.make_async_copy(served, served_hbm, sems.at[1])
    copy.start()
    copy.wait()
    here.wait()
    below.wait()


def shards(tokens, norm_gain, w_query, w_key, value_matrix, doc_lengths, block_server):
    rows, features = tokens.shape
    width = w_key.shape[1]
    heads = w_query.shape[1] // HEAD_SIZE
    block = QUERY_BLOCK_ROWS
    blocks = rows // block
    servers = lax.axis_size("attn")
    sharers = lax.axis_size("proj")
    chips = sharers // CORES
    me_attn = lax.axis_index("attn")
    me_proj = lax.axis_index("proj")
    sibling = [(i, i ^ 1) for i in range(sharers)]

    def across(distance):
        return [(i, (i + distance * CORES) % sharers) for i in range(sharers)]

    middle = blocks // 2
    chunks = [(middle * block, rows)] + [(i * block, (i + 1) * block) for i in reversed(range(middle))]
    arrived = []
    rest = tokens
    for low, high in chunks:
        piece = rest[low:high]
        if not arrived:
            piece, rest = lax.optimization_barrier((piece, rest))
        arrived.append([lax.ppermute(piece, "proj", across(d)) for d in range(1, chips)])
    other = lax.ppermute(tokens, "proj", sibling)

    order = [me_proj, me_proj ^ 1]
    for d in range(1, chips):
        source = (me_proj + sharers - d * CORES) % sharers
        order += [source, source ^ 1]
    order = jnp.stack([*order, me_attn * rows]).astype(jnp.int32)
    gains = norm_gain.reshape(sharers, features)

    w_key, value_matrix, w_query = [
        pltpu.with_memory_space_constraint(w, pltpu.HBM) for w in (w_key, value_matrix, w_query)
    ]
    q_acc, kv_acc, squares, bounds, routes, gain_rest, wkv_rest, wq_rest = local_part(
        order, doc_lengths, block_server, tokens, other, gains, w_key, value_matrix, w_query
    )

    onward = [(i, (i + 1) % servers) for i in range(servers)]
    own, prior, queries = [], [], []
    tie = kv_acc
    for (low, high), sources in zip(chunks, arrived):
        sources, tie = lax.optimization_barrier((sources, tie))
        cuts = range(0, high - low, 64)
        groups = []
        for piece in sources:
            pieces = [piece[i:j] for i, j in zip(cuts, [*cuts[1:], piece.shape[0]])]
            groups += [[piece], [lax.ppermute(part, "proj", sibling) for part in pieces]]
        rest = (high - low, low, groups, gain_rest, squares)
        kv, q = project(*rest, (wkv_rest, kv_acc), (wq_rest, q_acc))
        tie = q
        prior.append(lax.ppermute(kv, "attn", onward))
        own.append(kv)
        queries.append(q)

    queries = list(lax.optimization_barrier(tuple(queries)))

    operands = (*queries, *own)
    width = heads * HEAD_SIZE

    def results(count):
        return (
            jax.ShapeDtypeStruct((count * block, width), jnp.bfloat16),
            jax.ShapeDtypeStruct((count, heads, block), jnp.float32),
        )

    whole = jax.ShapeDtypeStruct((rows, width), jnp.bfloat16)
    kv_heads = w_key.shape[1] // HEAD_SIZE
    lanes = heads // kv_heads * block
    state_shapes = tuple(jax.ShapeDtypeStruct((kv_heads, n, lanes), jnp.float32) for n in (1, 1, HEAD_SIZE))
    above, above_lse, *states = pl.pallas_call(
        functools.partial(high_attention_kernel, chunks, list(range(middle, blocks))),
        out_shape=(*results(blocks - middle), *state_shapes),
        in_specs=[VMEM] * (len(operands) + 2),
        out_specs=(VMEM,) * 5,
        compiler_params=params(24 << 20),
        cost_estimate=cost(),
    )(*operands, prior[0], bounds)
    below, below_lse, *states, out = pl.pallas_call(
        functools.partial(low_attention_kernel, chunks, list(range(1, middle))),
        out_shape=(*results(middle - 1), *state_shapes, whole),
        in_specs=[VMEM] * (len(operands) + len(prior) + 4),
        out_specs=(VMEM,) * 5 + (HBM,),
        scratch_shapes=[pltpu.SemaphoreType.DMA],
        compiler_params=params(24 << 20),
        cost_estimate=cost(),
    )(*operands, *prior[:-1], bounds, above, *states)
    here, send = pl.pallas_call(
        functools.partial(last_attention_kernel, blocks, servers),
        out_shape=(results(1)[0], jax.ShapeDtypeStruct((servers, heads, block), jnp.bfloat16)),
        in_specs=[VMEM] * 9,
        out_specs=(VMEM, VMEM),
        scratch_shapes=[pltpu.VMEM((heads, block), jnp.float32)],
        compiler_params=params(24 << 20),
        cost_estimate=cost(),
    )(queries[-1], prior[-1], bounds, *states, routes, below_lse, above_lse)
    recv = lax.all_to_all(send, "attn", split_axis=0, concat_axis=0, tiled=True)
    served, out = pl.pallas_call(
        functools.partial(pick_kernel, blocks),
        out_shape=(
            jax.ShapeDtypeStruct((blocks, heads, block), jnp.float32),
            jax.ShapeDtypeStruct((rows, heads * HEAD_SIZE), jnp.bfloat16),
        ),
        in_specs=[VMEM, VMEM, VMEM, HBM],
        out_specs=(HBM, HBM),
        scratch_shapes=[pltpu.VMEM((blocks, heads, block), jnp.float32), pltpu.SemaphoreType.DMA((3,))],
        input_output_aliases={3: 1},
        compiler_params=params(),
    )(recv, here, below, out)
    return (out, served)


def solution(mesh):
    return jax.shard_map(
        shards,
        mesh=mesh,
        in_specs=(
            P("attn", "proj"),
            P(),
            P(None, "proj"),
            P(None, "proj"),
            P(None, "proj"),
            P(),
            P("attn"),
        ),
        out_specs=(P("attn", "proj"), P("attn", "proj", None)),
        check_vma=False,
    )
```

```python
import functools
import math

import jax
import jax.numpy as jnp
from jax import lax
from jax.experimental import pallas as pl
from jax.experimental.pallas import tpu as pltpu
from jax.sharding import PartitionSpec as P

HEAD_SIZE = 128
QUERY_BLOCK_ROWS = 128
CORES = 2

masked_value = -1e30
norm_eps = 1e-05
score_scale = 1.0 / HEAD_SIZE**0.5
log2_scale = score_scale * math.log2(math.e)

VMEM = pl.BlockSpec(memory_space=pltpu.VMEM)
SMEM = pl.BlockSpec(memory_space=pltpu.SMEM)
HBM = pl.BlockSpec(memory_space=pltpu.HBM)


def params(limit=16 << 20):
    return pltpu.CompilerParams(vmem_limit_bytes=limit)


def part_terms(x, gain):
    values = x.astype(jnp.float32)
    scaled = (values * gain).astype(jnp.bfloat16)
    return scaled, jnp.sum(values * values, axis=1, keepdims=True)


def cost():
    return pl.CostEstimate(flops=1 << 10, bytes_accessed=1 << 10, transcendentals=0)


def local_kernel(order_ref, docs_ref, server_ref, x_ref, other_ref, gain_ref, wk, wv, wq, *refs):
    q_ref, kv_ref, sq_ref, bound_ref, route_ref, gain_rest, kv_rest, q_rest, kv_own, q_own, sems = refs
    features, width = x_ref.shape[1], wk.shape[1]

    def fetch(slot, kv_to, q_to, place):
        rows = pl.ds(pl.multiple_of(order_ref[slot] * features, features), features)
        here = pl.ds(place * features, features)
        copies = (
            pltpu.make_async_copy(wk.at[rows, :], kv_to.at[here, pl.ds(0, width)], sems.at[slot, 0]),
            pltpu.make_async_copy(wv.at[rows, :], kv_to.at[here, pl.ds(width, width)], sems.at[slot, 1]),
            pltpu.make_async_copy(wq.at[rows, :], q_to.at[here, :], sems.at[slot, 2]),
        )
        for copy in copies:
            copy.start()
        return copies

    mine = [fetch(slot, kv_own, q_own, slot) for slot in range(CORES)]
    rest = [fetch(CORES + i, kv_rest, q_rest, i) for i in range(q_rest.shape[0] // features)]

    shape = bound_ref.shape
    base = order_ref[order_ref.shape[0] - 1]
    position = lax.broadcasted_iota(jnp.int32, shape, 0) * shape[1] + lax.broadcasted_iota(jnp.int32, shape, 1)
    start = -base
    bounds = jnp.full(shape, start, jnp.int32)
    for d in range(docs_ref.shape[0]):
        bounds = jnp.where(position >= start, start, bounds)
        start = start + docs_ref[d]
    bound_ref[...] = bounds
    for block in range(route_ref.shape[0]):
        route_ref[block] = jnp.full(route_ref.shape[1:], server_ref[block], jnp.int32)
    for i in range(gain_rest.shape[0]):
        gain_rest[i : i + 1, :] = gain_ref[pl.ds(order_ref[CORES + i], 1), :]

    parts = [
        part_terms(ref[...], gain_ref[pl.ds(order_ref[slot], 1), :]) for slot, ref in enumerate((x_ref, other_ref))
    ]
    sq_ref[...] = parts[0][1] + parts[1][1]
    scaled = jnp.concatenate([part[0] for part in parts], axis=1)
    for k, v, _ in mine:
        k.wait()
        v.wait()
    kv_ref[...] = jnp.dot(scaled, kv_own[...], preferred_element_type=jnp.float32)
    for _, _, q in mine:
        q.wait()
    q_ref[...] = jnp.dot(scaled, q_own[...], preferred_element_type=jnp.float32)
    for copies in rest:
        for copy in copies:
            copy.wait()


def local_part(order, docs, block_server, x, other, gains, wk, wv, wq):
    rows, features = x.shape
    q_width, kv_width = wq.shape[1], 2 * wk.shape[1]
    rest = wq.shape[0] - CORES * features
    return pl.pallas_call(
        local_kernel,
        out_shape=(
            pltpu.VMEM((rows, q_width), jnp.float32),
            pltpu.VMEM((rows, kv_width), jnp.float32),
            pltpu.VMEM((rows, 1), jnp.float32),
            pltpu.VMEM((rows // QUERY_BLOCK_ROWS, QUERY_BLOCK_ROWS), jnp.int32),
            pltpu.VMEM((rows // QUERY_BLOCK_ROWS, q_width // HEAD_SIZE, QUERY_BLOCK_ROWS), jnp.int32),
            pltpu.VMEM((rest // features, features), jnp.float32),
            pltpu.VMEM((rest, kv_width), jnp.bfloat16),
            pltpu.VMEM((rest, q_width), jnp.bfloat16),
        ),
        in_specs=[SMEM, SMEM, SMEM, VMEM, VMEM, VMEM, HBM, HBM, HBM],
        out_specs=(VMEM,) * 8,
        scratch_shapes=[
            pltpu.VMEM((CORES * features, kv_width), jnp.bfloat16),
            pltpu.VMEM((CORES * features, q_width), jnp.bfloat16),
            pltpu.SemaphoreType.DMA((wq.shape[0] // features, 3)),
        ],
        compiler_params=params(32 << 20),
        cost_estimate=cost(),
    )(order, docs, block_server, x, other, gains, wk, wv, wq)


def remote_rows(sizes, refs, gain_ref):
    terms = []
    for i, size in enumerate(sizes):
        x = jnp.concatenate([ref[...] for ref in refs[:size]], axis=0)
        refs = refs[size:]
        terms.append(part_terms(x, gain_ref[i : i + 1, :]))
    return jnp.concatenate([x for x, _ in terms], axis=1), sum(square for _, square in terms)


def chunk_kernel(sizes, row, kinds, *refs):
    pieces, (gain_ref, sq_ref, *refs) = refs[: sum(sizes)], refs[sum(sizes) :]
    scaled, squares = remote_rows(sizes, pieces, gain_ref)
    here = slice(row, row + scaled.shape[0])
    features = scaled.shape[1] // len(sizes)
    inverse = lax.rsqrt((sq_ref[here, :] + squares) / (features * (len(sizes) + CORES)) + norm_eps)
    for i in range(kinds):
        w_ref, acc_ref = refs[2 * i : 2 * i + 2]
        total = acc_ref[here, :] + jnp.dot(scaled, w_ref[...], preferred_element_type=jnp.float32)
        refs[2 * kinds + i][...] = (total * inverse).astype(jnp.bfloat16)


def project(rows, row, groups, gains, squares, *sides):
    operands = [piece for group in groups for piece in group] + [gains, squares]
    for side in sides:
        operands += side
    return pl.pallas_call(
        functools.partial(chunk_kernel, [len(group) for group in groups], row, len(sides)),
        out_shape=tuple(jax.ShapeDtypeStruct((rows, w.shape[1]), jnp.bfloat16) for w, _ in sides),
        in_specs=[VMEM] * len(operands),
        out_specs=(VMEM,) * len(sides),
        compiler_params=params(),
        cost_estimate=cost(),
    )(*operands)


def block_parts(refs, chunks):
    found = {}
    block = QUERY_BLOCK_ROWS
    for i in range(chunks[0][1] // block):
        parts = []
        for ref, (low, high) in zip(refs, chunks):
            first, last = max(low, i * block), min(high, (i + 1) * block)
            if first < last:
                parts.insert(0, (ref, first - low, last - low))
        if sum(last - first for _, first, last in parts) == block:
            found[i] = parts
    return found


def score_caps(bounds, key_starts, row_start):
    rows = QUERY_BLOCK_ROWS
    query_pos = row_start + lax.broadcasted_iota(jnp.int32, (rows, rows), 1)
    caps = []
    for start in key_starts:
        key_pos = start + lax.broadcasted_iota(jnp.int32, (rows, rows), 0)
        ok = key_pos >= bounds
        if start == row_start:
            ok = ok & (key_pos <= query_pos)
        caps.append(jnp.where(ok, jnp.inf, masked_value))
    return jnp.concatenate(caps, axis=0)


def attend_blocks(wanted, blocks, queries, owns, priors, bounds_ref, outs, lse_refs, states=()):
    rows = QUERY_BLOCK_ROWS
    width = owns[wanted[0]][0][0].shape[1] // 2
    kv_heads, group = width // HEAD_SIZE, outs[wanted[0]][0].shape[1] // width
    keys, caps = {}, {}
    for b in wanted:
        before = [i for i in range(b, blocks) if i in priors]
        keys[b] = [part for i in before for part in priors[i]] + [part for i in range(b + 1) for part in owns[i]]
        starts = [(i - blocks) * rows for i in before] + [i * rows for i in range(b + 1)]
        caps[b] = jnp.concatenate([score_caps(bounds_ref[b : b + 1, :], starts, b * rows)] * group, axis=1)
    steps = [(b, n) for b in wanted for n in range(kv_heads)]

    def columns(parts, first):
        return jnp.concatenate([ref[i:j, first : first + HEAD_SIZE] for ref, i, j in parts], axis=0)

    def score(b, n):
        heads = range(n * group, (n + 1) * group)
        stacked = jnp.concatenate([columns(queries[b], h * HEAD_SIZE) for h in heads], axis=0)
        return lax.dot_general(
            columns(keys[b], n * HEAD_SIZE), stacked, (((1,), (1,)), ((), ())), preferred_element_type=jnp.float32
        )

    def weigh(b, scores):
        scores = jnp.minimum(scores, caps[b])
        highest = jnp.max(scores, axis=0, keepdims=True)
        return highest, jnp.exp2((scores - highest) * log2_scale)

    def finish(b, n, highest, weights):
        total = jnp.sum(weights, axis=0, keepdims=True)
        summed = lax.dot_general(
            columns(keys[b], width + n * HEAD_SIZE),
            weights.astype(jnp.bfloat16),
            (((0,), (0,)), ((), ())),
            preferred_element_type=jnp.float32,
        )
        if b == 0:
            for ref, value in zip(states, (highest, total, summed)):
                ref[n] = value
            return
        result = (summed / total).astype(jnp.bfloat16)
        lse = highest * score_scale + jnp.log(total)
        ref, at = outs[b]
        for g in range(group):
            h, part = n * group + g, slice(g * rows, (g + 1) * rows)
            ref[at : at + rows, h * HEAD_SIZE : (h + 1) * HEAD_SIZE] = jnp.transpose(result[:, part])
            lse_refs[b][h : h + 1, :] = lse[:, part]

    scores, pending = score(*steps[0]), None
    for i, (b, n) in enumerate(steps):
        ahead = score(*steps[i + 1]) if i + 1 < len(steps) else None
        highest, weights = weigh(b, scores)
        if pending is not None:
            finish(*pending)
        pending, scores = (b, n, highest, weights), ahead
    finish(*pending)


def attention_refs(chunks, refs):
    count = len(chunks)
    queries = block_parts(refs[:count], chunks)
    owns = block_parts(refs[count : 2 * count], chunks)
    return queries, owns, refs[2 * count :]


def merge_keys(n, prior_parts, query_parts, caps, states):
    width = prior_parts[0][0].shape[1] // 2
    group = query_parts[0][0].shape[1] // width

    def columns(parts, first):
        return jnp.concatenate([ref[i:j, first : first + HEAD_SIZE] for ref, i, j in parts], axis=0)

    heads = range(n * group, (n + 1) * group)
    stacked = jnp.concatenate([columns(query_parts, h * HEAD_SIZE) for h in heads], axis=0)
    scores = lax.dot_general(
        columns(prior_parts, n * HEAD_SIZE), stacked, (((1,), (1,)), ((), ())), preferred_element_type=jnp.float32
    )
    scores = jnp.minimum(scores, caps)
    highest, total, summed = (ref[n] for ref in states)
    top = jnp.maximum(highest, jnp.max(scores, axis=0, keepdims=True))
    weights = jnp.exp2((scores - top) * log2_scale)
    scale = jnp.exp2((highest - top) * log2_scale)
    total = total * scale + jnp.sum(weights, axis=0, keepdims=True)
    summed = summed * scale + lax.dot_general(
        columns(prior_parts, width + n * HEAD_SIZE),
        weights.astype(jnp.bfloat16),
        (((0,), (0,)), ((), ())),
        preferred_element_type=jnp.float32,
    )
    return top, total, summed


def prior_caps(bounds_ref, block, blocks, group):
    starts = [(block - blocks) * QUERY_BLOCK_ROWS]
    return jnp.concatenate([score_caps(bounds_ref[:1, :], starts, 0)] * group, axis=1)


def high_attention_kernel(chunks, wanted, *refs):
    queries, owns, refs = attention_refs(chunks, refs)
    prior_ref, bounds_ref, out_ref, lse_ref, *states = refs
    priors = block_parts([prior_ref], chunks)
    low, blocks = wanted[0], chunks[0][1] // QUERY_BLOCK_ROWS
    outs = {b: (out_ref, (b - low) * QUERY_BLOCK_ROWS) for b in wanted}
    lses = {b: lse_ref.at[b - low] for b in wanted}
    attend_blocks([*wanted, 0], blocks, queries, owns, priors, bounds_ref, outs, lses, states)


def low_attention_kernel(chunks, wanted, *refs):
    queries, owns, refs = attention_refs(chunks, refs)
    *refs, out_hbm, sem = refs
    *refs, out_ref, lse_ref, highest_ref, total_ref, summed_ref = refs
    *priors, bounds_ref, above_ref, highest, total, summed = refs
    priors = block_parts(priors, chunks)
    rows = pl.ds((wanted[-1] + 1) * QUERY_BLOCK_ROWS, above_ref.shape[0])
    copy = pltpu.make_async_copy(above_ref, out_hbm.at[rows, :], sem)
    copy.start()
    outs = {b: (out_ref, (b - wanted[0]) * QUERY_BLOCK_ROWS) for b in wanted}
    lses = {b: lse_ref.at[b - wanted[0]] for b in wanted}
    blocks = chunks[0][1] // QUERY_BLOCK_ROWS
    attend_blocks(wanted, blocks, queries, owns, priors, bounds_ref, outs, lses)
    kv_heads = highest.shape[0]
    group = highest.shape[2] // QUERY_BLOCK_ROWS
    states = (highest, total, summed)
    for b in wanted:
        caps = prior_caps(bounds_ref, b, blocks, group)
        merged = [merge_keys(n, priors[b], queries[0], caps, states) for n in range(kv_heads)]
        states = (highest_ref, total_ref, summed_ref)
        for n, values in enumerate(merged):
            for ref, value in zip(states, values):
                ref[n] = value
    copy.wait()


def last_attention_kernel(blocks, servers, q_ref, prior_ref, bounds_ref, *refs):
    *states, route_ref, below_lse, above_lse, here, send_ref, lse_ref = refs
    block = QUERY_BLOCK_ROWS
    kv_heads = states[0].shape[0]
    group = states[0].shape[2] // block
    caps = prior_caps(bounds_ref, 0, blocks, group)
    merged = [merge_keys(n, [(prior_ref, 0, block)], [(q_ref, 0, block)], caps, states) for n in range(kv_heads)]
    for n, (highest, total, summed) in enumerate(merged):
        result = (summed / total).astype(jnp.bfloat16)
        lse = highest * score_scale + jnp.log(total)
        for g in range(group):
            h, part = n * group + g, slice(g * block, (g + 1) * block)
            here[:, h * HEAD_SIZE : (h + 1) * HEAD_SIZE] = jnp.transpose(result[:, part])
            lse_ref[h : h + 1, :] = lse[:, part]
    lses = [lse_ref[...]] + [ref[i] for ref in (below_lse, above_lse) for i in range(ref.shape[0])]
    for s in range(servers):
        value = jnp.full(lses[0].shape, jnp.inf, jnp.float32)
        for i, rows in enumerate(lses):
            value = jnp.where(route_ref[i] == s, rows, value)
        send_ref[s] = value.astype(jnp.bfloat16)


def pick_kernel(blocks, recv_ref, here_ref, below_ref, _, served_hbm, out_hbm, served, sems):
    here = pltpu.make_async_copy(here_ref, out_hbm.at[pl.ds(0, here_ref.shape[0]), :], sems.at[0])
    here.start()
    rows = pl.ds(here_ref.shape[0], below_ref.shape[0])
    below = pltpu.make_async_copy(below_ref, out_hbm.at[rows, :], sems.at[2])
    below.start()
    shape = recv_ref.shape[1:]
    rank = jnp.zeros(shape, jnp.int32)
    picked = [jnp.zeros(shape, jnp.float32) for _ in range(blocks)]
    for i in range(recv_ref.shape[0]):
        value = recv_ref[i].astype(jnp.float32)
        valid = value < jnp.inf
        for k in range(blocks):
            picked[k] = jnp.where(valid & (rank == k), value, picked[k])
        rank = rank + valid.astype(jnp.int32)
    for k in range(blocks):
        served[k] = picked[k]
    copy = pltpu.make_async_copy(served, served_hbm, sems.at[1])
    copy.start()
    copy.wait()
    here.wait()
    below.wait()


def shards(tokens, norm_gain, w_query, w_key, value_matrix, doc_lengths, block_server):
    rows, features = tokens.shape
    width = w_key.shape[1]
    heads = w_query.shape[1] // HEAD_SIZE
    block = QUERY_BLOCK_ROWS
    blocks = rows // block
    servers = lax.axis_size("attn")
    sharers = lax.axis_size("proj")
    chips = sharers // CORES
    me_attn = lax.axis_index("attn")
    me_proj = lax.axis_index("proj")
    sibling = [(i, i ^ 1) for i in range(sharers)]

    def across(distance):
        return [(i, (i + distance * CORES) % sharers) for i in range(sharers)]

    middle = blocks // 2
    chunks = [(middle * block, rows)] + [(i * block, (i + 1) * block) for i in reversed(range(middle))]
    arrived = []
    rest = tokens
    for low, high in chunks:
        piece = rest[low:high]
        if not arrived:
            piece, rest = lax.optimization_barrier((piece, rest))
        arrived.append([lax.ppermute(piece, "proj", across(d)) for d in range(1, chips)])
    other = lax.ppermute(tokens, "proj", sibling)

    order = [me_proj, me_proj ^ 1]
    for d in range(1, chips):
        source = (me_proj + sharers - d * CORES) % sharers
        order += [source, source ^ 1]
    order = jnp.stack([*order, me_attn * rows]).astype(jnp.int32)
    gains = norm_gain.reshape(sharers, features)

    w_key, value_matrix, w_query = [
        pltpu.with_memory_space_constraint(w, pltpu.HBM) for w in (w_key, value_matrix, w_query)
    ]
    q_acc, kv_acc, squares, bounds, routes, gain_rest, wkv_rest, wq_rest = local_part(
        order, doc_lengths, block_server, tokens, other, gains, w_key, value_matrix, w_query
    )

    onward = [(i, (i + 1) % servers) for i in range(servers)]
    own, prior, queries = [], [], []
    tie = kv_acc
    for (low, high), sources in zip(chunks, arrived):
        sources, tie = lax.optimization_barrier((sources, tie))
        cuts = range(0, high - low, 64)
        groups = []
        for piece in sources:
            pieces = [piece[i:j] for i, j in zip(cuts, [*cuts[1:], piece.shape[0]])]
            groups += [[piece], [lax.ppermute(part, "proj", sibling) for part in pieces]]
        rest = (high - low, low, groups, gain_rest, squares)
        kv, q = project(*rest, (wkv_rest, kv_acc), (wq_rest, q_acc))
        tie = q
        prior.append(lax.ppermute(kv, "attn", onward))
        own.append(kv)
        queries.append(q)

    queries = list(lax.optimization_barrier(tuple(queries)))

    operands = (*queries, *own)
    width = heads * HEAD_SIZE

    def results(count):
        return (
            jax.ShapeDtypeStruct((count * block, width), jnp.bfloat16),
            jax.ShapeDtypeStruct((count, heads, block), jnp.float32),
        )

    whole = jax.ShapeDtypeStruct((rows, width), jnp.bfloat16)
    kv_heads = w_key.shape[1] // HEAD_SIZE
    lanes = heads // kv_heads * block
    state_shapes = tuple(jax.ShapeDtypeStruct((kv_heads, n, lanes), jnp.float32) for n in (1, 1, HEAD_SIZE))
    above, above_lse, *states = pl.pallas_call(
        functools.partial(high_attention_kernel, chunks, list(range(middle, blocks))),
        out_shape=(*results(blocks - middle), *state_shapes),
        in_specs=[VMEM] * (len(operands) + 2),
        out_specs=(VMEM,) * 5,
        compiler_params=params(24 << 20),
        cost_estimate=cost(),
    )(*operands, prior[0], bounds)
    below, below_lse, *states, out = pl.pallas_call(
        functools.partial(low_attention_kernel, chunks, list(range(1, middle))),
        out_shape=(*results(middle - 1), *state_shapes, whole),
        in_specs=[VMEM] * (len(operands) + len(prior) + 4),
        out_specs=(VMEM,) * 5 + (HBM,),
        scratch_shapes=[pltpu.SemaphoreType.DMA],
        compiler_params=params(24 << 20),
        cost_estimate=cost(),
    )(*operands, *prior[:-1], bounds, above, *states)
    here, send = pl.pallas_call(
        functools.partial(last_attention_kernel, blocks, servers),
        out_shape=(results(1)[0], jax.ShapeDtypeStruct((servers, heads, block), jnp.bfloat16)),
        in_specs=[VMEM] * 9,
        out_specs=(VMEM, VMEM),
        scratch_shapes=[pltpu.VMEM((heads, block), jnp.float32)],
        compiler_params=params(24 << 20),
        cost_estimate=cost(),
    )(queries[-1], prior[-1], bounds, *states, routes, below_lse, above_lse)
    recv = lax.all_to_all(send, "attn", split_axis=0, concat_axis=0, tiled=True)
    served, out = pl.pallas_call(
        functools.partial(pick_kernel, blocks),
        out_shape=(
            jax.ShapeDtypeStruct((blocks, heads, block), jnp.float32),
            jax.ShapeDtypeStruct((rows, heads * HEAD_SIZE), jnp.bfloat16),
        ),
        in_specs=[VMEM, VMEM, VMEM, HBM],
        out_specs=(HBM, HBM),
        scratch_shapes=[pltpu.VMEM((blocks, heads, block), jnp.float32), pltpu.SemaphoreType.DMA((3,))],
        input_output_aliases={3: 1},
        compiler_params=params(),
    )(recv, here, below, out)
    return (out, served)


def solution(mesh):
    return jax.shard_map(
        shards,
        mesh=mesh,
        in_specs=(
            P("attn", "proj"),
            P(),
            P(None, "proj"),
            P(None, "proj"),
            P(None, "proj"),
            P(),
            P("attn"),
        ),
        out_specs=(P("attn", "proj"), P("attn", "proj", None)),
        check_vma=False,
    )
```
